512 devices in a mesh: dp: 16 (over x, z_lo, core), fsdp: 32 (over y, z_hi).
Axes of the slice: x: 4, y: 8, z: 8 (z_hi: 4, z_lo: 2; z = z_hi * 2 + z_lo), core: 2. Of those that a mesh axis runs over, the one named last changes fastest.
Arguments:
- tokens: bfloat16 [2048, 4096], P(('dp', 'fsdp')), may hold values from -6 to 6
- cotangent: bfloat16 [2048, 4096], P(('dp', 'fsdp')), may hold values from -6 to 6
- w_in: bfloat16 [1152, 128, 128], P('fsdp'), may hold values from -0.1875 to 0.1875
- w_out: bfloat16 [1152, 128, 128], P('fsdp'), may hold values from -0.09375 to 0.09375
- in_rows: int32 [1152], P('fsdp'), may hold values from -1 to 127, as said below
- in_cols: int32 [1152], P('fsdp'), may hold values from -1 to 31, as said below
- out_rows: int32 [1152], P('fsdp'), may hold values from -1 to 127, as said below
- out_cols: int32 [1152], P('fsdp'), may hold values from -1 to 31, as said below
Outputs:
- mixed: bfloat16 [2048, 4096], P(('dp', 'fsdp'))
- input_grad: bfloat16 [2048, 4096], P(('dp', 'fsdp'))
- in_grad: bfloat16 [1152, 128, 128], P('fsdp')
- out_grad: bfloat16 [1152, 128, 128], P('fsdp')
The draws below stay inside these ranges and needn't reach their ends.
Inputs may be any that keep to these rules, and one draw needn't show every extreme that they name: `in_rows`: slot s lies on fsdp device s // 36. A live slot names a hidden panel r with r // 4 equal to that device; -1 marks an empty slot, and empty slots follow the live ones of their device. No (panel, column block) pair is named twice. On some device all 36 slots are live, on every device at least 24. `in_cols`: -1 exactly where in_rows is -1. `out_rows`: as in_rows, for w_out. `out_cols`: -1 exactly where out_rows is -1.
All inputs are finite; a program needn't handle non-finite values.
Results may differ from the reference program's by a relative error of at most 0.025.
Values may be sent and summed in bfloat16 or wider, within the bound.
A program may use at most 64 MiB of HBM per device.

```python
import jax
import jax.numpy as jnp
from jax import lax

D = 4096
FF = 16384
BLK_PAN = 9
NCB = 32
PAN_DEV = 4
CAP = 36
NBLK = 1152
TOK_GROUP = 128
TOKENS = 2048
N_DP = 16
N_FSDP = 32


def block_layout(key, tag):
    npanel = FF // 128
    ncol = D // 128
    ndev = npanel // PAN_DEV
    sub_key = jax.random.fold_in(key, tag)
    forced = jax.random.randint(jax.random.fold_in(sub_key, 1), (), 0, ndev)
    totals = CAP - jax.random.randint(jax.random.fold_in(sub_key, 2), (ndev,), 0, CAP // 3 + 1)
    totals = jnp.where(jnp.arange(ndev) == forced, CAP, totals)

    def one_device(device):
        positions = jax.random.permutation(jax.random.fold_in(sub_key, 100 + device), PAN_DEV * ncol)[:CAP]
        local_panel = positions // ncol
        column = positions % ncol
        panel_index = device * PAN_DEV + local_panel
        is_live = jnp.arange(CAP) < totals[device]
        return (jnp.where(is_live, panel_index, -1), jnp.where(is_live, column, -1))
    panels, columns = jax.vmap(one_device)(jnp.arange(ndev))
    return (panels.reshape(-1).astype(jnp.int32), columns.reshape(-1).astype(jnp.int32))


def draw_in_rows(key, part):
    return block_layout(key, 11)[0]


def draw_in_cols(key, part):
    return block_layout(key, 11)[1]


def draw_out_rows(key, part):
    return block_layout(key, 23)[0]


def draw_out_cols(key, part):
    return block_layout(key, 23)[1]


def level_of(rng, extent, shards, smallest, top_value):
    gain, own = 1.0, jax.random.fold_in(rng, 6)
    for axis_at, blocks in shards:
        heights = jnp.exp(jax.random.uniform(jax.random.fold_in(own, axis_at), (blocks,), jnp.float32, smallest / len(shards), top_value / len(shards)))
        gain = gain * jnp.repeat(heights, extent[axis_at] // blocks).reshape([-1 if axis == axis_at else 1 for axis in range(len(extent))])
    return gain


def scatter_about(rng, dims, scale, reach, split=(), kind=jnp.bfloat16):
    values = scale * jax.random.normal(rng, dims, jnp.float32)
    if split:
        values = values * level_of(rng, dims, split, -0.22, 0.18)
    return jnp.clip(values, -reach, reach).astype(kind)


def setup_inputs(seed: int = 0) -> dict:
    arg_keys = jax.random.split(jax.random.key(seed), 9)
    tokens = scatter_about(arg_keys[0], (TOKENS, D), 1.0, 6.0, ((0, 512),))
    cotangent = scatter_about(arg_keys[1], (TOKENS, D), 1.0, 6.0, ((0, 512),))
    w_in = scatter_about(arg_keys[2], (NBLK, 128, 128), (BLK_PAN * 128) ** -0.5, 0.1875, ((0, 32),))
    w_out = scatter_about(arg_keys[3], (NBLK, 128, 128), (CAP * N_FSDP * 128 // NCB) ** -0.5, 0.09375, ((0, 32),))
    in_rows = draw_in_rows(jax.random.fold_in(arg_keys[8], 71), 0)
    in_cols = draw_in_cols(jax.random.fold_in(arg_keys[8], 71), 0)
    out_rows = draw_out_rows(jax.random.fold_in(arg_keys[8], 71), 0)
    out_cols = draw_out_cols(jax.random.fold_in(arg_keys[8], 71), 0)
    return {"tokens": tokens, "cotangent": cotangent, "w_in": w_in, "w_out": w_out, "in_rows": in_rows, "in_cols": in_cols, "out_rows": out_rows, "out_cols": out_cols}


def gelu_slope(values):
    cdf = 0.5 * (1.0 + jax.scipy.special.erf(values * 0.7071067811865476))
    return cdf + values * jnp.exp(-0.5 * values * values) * 0.3989422804014327


def dense_grid(blocks, slot_rows, slot_cols):
    npanel = FF // 128
    ncol = D // 128
    is_live = slot_rows >= 0
    row_index = jnp.where(is_live, slot_rows, 0).astype(jnp.int32)
    col_index = jnp.where(is_live, slot_cols, 0).astype(jnp.int32)
    kept = jnp.where(is_live[:, None, None], blocks, jnp.zeros_like(blocks))
    block_grid = jnp.zeros((npanel, ncol, 128, 128), blocks.dtype).at[row_index, col_index].add(kept)
    return block_grid.transpose(0, 2, 1, 3).reshape(FF, D)


def extract_blocks(full_grad, slot_rows, slot_cols):
    npanel = FF // 128
    ncol = D // 128
    is_live = slot_rows >= 0
    row_index = jnp.where(is_live, slot_rows, 0).astype(jnp.int32)
    col_index = jnp.where(is_live, slot_cols, 0).astype(jnp.int32)
    shaped = full_grad.reshape(npanel, 128, ncol, 128)
    picked = shaped[row_index, :, col_index, :]
    return jnp.where(is_live[:, None, None], picked, jnp.zeros_like(picked))


def round_trip(values):
    return lax.optimization_barrier(values.astype(jnp.bfloat16)).astype(jnp.float32)


def reference(tokens, cotangent, w_in, w_out, in_rows, in_cols, out_rows, out_cols):
    npanel = FF // 128
    ndev = npanel // PAN_DEV
    dense_in = dense_grid(w_in, in_rows, in_cols)
    dense_out = dense_grid(w_out, out_rows, out_cols)
    owner_in = dense_in.reshape(ndev, PAN_DEV * 128, D).astype(jnp.float32)
    owner_out = dense_out.reshape(ndev, PAN_DEV * 128, D).astype(jnp.float32)

    def by_owner(acts, owner_weight):
        parts = acts.reshape(TOK_GROUP, ndev, PAN_DEV * 128)
        partial_value = jnp.einsum('tnk,nkd->ntd', parts.astype(jnp.float32), owner_weight)
        return jnp.sum(round_trip(partial_value), axis=0).astype(jnp.bfloat16)

    def group_step(grad_totals, group_data):
        rows_x, rows_dy = group_data
        pre_act = jnp.dot(rows_x, dense_in.T, preferred_element_type=jnp.float32)
        hidden = jax.nn.gelu(pre_act, approximate=False).astype(jnp.bfloat16)
        mixed = by_owner(hidden, owner_out)
        d_hidden = jnp.dot(rows_dy, dense_out.T, preferred_element_type=jnp.float32)
        d_pre = (d_hidden * gelu_slope(pre_act)).astype(jnp.bfloat16)
        input_grad = by_owner(d_pre, owner_in)
        grad_out = extract_blocks(jnp.dot(hidden.T, rows_dy, preferred_element_type=jnp.float32), out_rows, out_cols)
        grad_in = extract_blocks(jnp.dot(d_pre.T, rows_x, preferred_element_type=jnp.float32), in_rows, in_cols)
        total_in, total_out = grad_totals
        return (total_in + round_trip(grad_in), total_out + round_trip(grad_out)), (mixed, input_grad)

    start = (jnp.zeros((NBLK, 128, 128), jnp.float32), jnp.zeros((NBLK, 128, 128), jnp.float32))
    group_x = tokens.reshape(N_DP, TOK_GROUP, D)
    group_dy = cotangent.reshape(N_DP, TOK_GROUP, D)
    totals, outputs = lax.scan(group_step, start, (group_x, group_dy))
    mixed = outputs[0].reshape(TOKENS, D)
    input_grad = outputs[1].reshape(TOKENS, D)
    return mixed, input_grad, totals[0].astype(jnp.bfloat16), totals[1].astype(jnp.bfloat16)
```

```python
import jax
import jax.numpy as jnp
from jax import lax
from jax.experimental import pallas as pl
from jax.experimental.pallas import tpu as pltpu
from jax.sharding import PartitionSpec as P

MESH = pl.DeviceIdType.MESH
F32 = jnp.float32
BF16 = jnp.bfloat16

NY, NZ = 8, 4
CAP = 36
NCOL = 32
NPAN = 4
D = 4096
SEMS = 96


def mo(v, m=16):
    return pl.multiple_of(v, m)


def kernel(
    tok, cot, w_in, w_out, tab,
    mixed_o, igrad_o, ing_o, outg_o,
    x, zb, t1, t2, ws, wd, xb, hd, prt, rland, lland, zs, zl, g, fo, lc, l1, l2, l3,
    ssem, rsem, lsem,
):
    dp, fs = lax.axis_index("dp"), lax.axis_index("fsdp")
    y, zh = fs // NZ, fs % NZ
    px, zlo, core = dp // 4, (dp // 2) % 2, dp % 2

    def dev(d=dp, f=fs):
        return (d, f)

    z_peers = [(zh + d) % NZ for d in (1, 2, 3)]
    z_devs = [dev(f=y * NZ + j) for j in z_peers]
    right = dev(f=((y + 1) % NY) * NZ + zh)
    left = dev(f=((y + NY - 1) % NY) * NZ + zh)
    core_dev = dev(d=dp + 1 - 2 * core)
    xpa = px + 1 - 2 * (px % 2)
    xpb = (px + 2 * (px % 2) + 3) % 4
    xa_dev = dev(d=xpa * 4 + dp % 4)
    xb_dev = dev(d=xpb * 4 + dp % 4)
    zlo_dev = dev(d=dp + 2 - 4 * zlo)
    everyone = [*z_devs, right, left, core_dev, xa_dev, xb_dev, zlo_dev]

    used = [0]
    started = []

    def send(src, dst, to):
        i = used[0]
        used[0] += 1
        c = pltpu.make_async_remote_copy(
            src, dst, ssem.at[i], rsem.at[i], device_id=to, device_id_type=MESH
        )
        c.start()
        started.append(c)
        return c

    weights = [
        pltpu.make_async_copy(w, ws.at[a, pl.ds(0, CAP)], lsem.at[a])
        for a, w in enumerate((w_in, w_out))
    ]
    for c in weights:
        c.start()

    barrier = pltpu.get_barrier_semaphore()
    for to in everyone:
        pl.semaphore_signal(barrier, inc=1, device_id=to, device_id_type=MESH)

    for a, src in enumerate((tok, cot)):
        rows = src[...].astype(F32)
        for k in range(4):
            t1[a, 4 * k : 4 * k + 4, :] = rows[:, 1024 * k : 1024 * (k + 1)]
        zb[a, zh] = t1[a].astype(BF16)
    ws[0, CAP] = jnp.zeros((128, 128), BF16)
    ws[1, CAP] = jnp.zeros((128, 128), BF16)
    hd[0, NPAN] = jnp.zeros((128, 128), BF16)
    hd[1, NPAN] = jnp.zeros((128, 128), BF16)

    pl.semaphore_wait(barrier, len(everyone))

    zsend = [[send(zb.at[a, zh], zb.at[a, zh], to) for to in z_devs] for a in range(2)]

    def unfold(a):
        for j in range(NZ):
            t1[a] = zb[a, j].astype(F32)
            for k in range(4):
                t2[a, 4 * j : 4 * j + 4, 1024 * k : 1024 * (k + 1)] = t1[a, 4 * k : 4 * k + 4, :]
        x[a, y] = t2[a].astype(BF16)

    rights, lefts = (4, 3), (3, 4)
    chain_r, chain_l = [[], []], [[], []]

    def hop(a, k):
        if k < rights[a]:
            if k:
                chain_r[a][k - 1].wait_recv()
            b = (y + NY - k) % NY
            chain_r[a].append(send(x.at[a, b], x.at[a, b], right))
        if k < lefts[a]:
            if k:
                chain_l[a][k - 1].wait_recv()
            b = (y + k) % NY
            chain_l[a].append(send(x.at[a, b], x.at[a, b], left))

    def dense(a):
        if a == 0:
            for w in weights:
                w.wait()

        def one(c, _):
            for p in range(NPAN):
                slot = tab[a, p * NCOL + c]
                wd[a, pl.ds(p * 128, 128), pl.ds(mo(c * 128, 128), 128)] = ws[a, slot]
            return 0

        lax.fori_loop(0, NCOL, one, 0)

    for a in range(2):
        for c in zsend[a]:
            c.wait_recv()
        unfold(a)
        hop(a, 0)
    dense(0)
    hop(0, 1)
    hop(1, 1)
    dense(1)
    for k in (2, 3):
        hop(0, k)
        hop(1, k)
    for a in range(2):
        chain_r[a][-1].wait_recv()
        chain_l[a][-1].wait_recv()

    nt = (((1,), (1,)), ((), ()))

    def by_panel(a):
        return lax.dot_general(wd[a], x[a].reshape(128, D), nt, preferred_element_type=F32)

    def blocks(a):
        def one(c, _):
            xb[a, c] = x[a, :, :, pl.ds(mo(c * 128, 128), 128)].reshape(128, 128)
            return 0

        lax.fori_loop(0, NCOL, one, 0)

    def grads(dst, a, t, side):
        def one(s, _):
            panel = tab[t, 128 + s]
            col = tab[t, 128 + CAP + s]
            blk = jnp.dot(hd[side, panel], xb[a, col], preferred_element_type=F32)
            g[dst, pl.ds(mo(s * 128, 128), 128), :] = blk.astype(BF16)
            return 0

        lax.fori_loop(0, CAP, one, 0, unroll=4)

    def partial(dst, side, a):
        acts = hd[side, :NPAN].reshape(512, 128).astype(F32).T.astype(BF16)

        def one(n, _):
            cols = pl.ds(mo(n * 512, 512), 512)
            part = jnp.dot(acts, wd[a, :, cols], preferred_element_type=F32)
            prt[dst, :, :, cols] = part.astype(BF16).reshape(NY, 16, 512)
            return 0

        lax.fori_loop(0, D // 512, one, 0)

    def scatter(a):
        nr, nl = rights[a], lefts[a]
        rc = [send(prt.at[a, (y + nr) % NY], rland.at[a, 0], right)]
        lc_ = [send(prt.at[a, (y + NY - nl) % NY], lland.at[a, 0], left)]
        for k in range(1, 4):
            for chain, land, n, to, sign in (
                (rc, rland, nr, right, 1),
                (lc_, lland, nl, left, NY - 1),
            ):
                if k >= n:
                    continue
                yield
                chain[k - 1].wait_recv()
                own = prt[a, (y + sign * (n - k)) % NY].astype(F32)
                land[a, k - 1] = (own + land[a, k - 1].astype(F32)).astype(BF16)
                chain.append(send(land.at[a, k - 1], land.at[a, k], to))
        yield
        rc[-1].wait_recv()
        lc_[-1].wait_recv()
        t2[a] = (
            prt[a, y].astype(F32)
            + rland[a, nr - 1].astype(F32)
            + lland[a, nl - 1].astype(F32)
        )
        for j in range(NZ):
            for k in range(4):
                t1[a, 4 * k : 4 * k + 4, :] = t2[a, 4 * j : 4 * j + 4, 1024 * k : 1024 * (k + 1)]
            zs[a, j] = t1[a].astype(BF16)
        out = [send(zs.at[a, j], zl.at[a, zh], to) for j, to in zip(z_peers, z_devs)]
        yield
        for c in out:
            c.wait_recv()
        total = zs[a, zh].astype(F32)
        for j in z_peers:
            total = total + zl[a, j].astype(F32)
        t1[a] = total
        dst = (mixed_o, igrad_o)[a]
        for k in range(4):
            dst[:, 1024 * k : 1024 * (k + 1)] = t1[a, 4 * k : 4 * k + 4, :].astype(BF16)

    ha1, ha2 = ((px + 1) // 2) % 2, px // 2
    hb1, hb2 = px // 2, px % 2
    base = core * 2304
    other = 2304 - base
    ra1 = base + ha1 * 576
    sa1 = base + 576 - ha1 * 576
    ra2 = ra1 + ha2 * 288
    sa2 = ra1 + 288 - ha2 * 288
    rb1 = base + 1152 + hb1 * 576
    sb1 = base + 1152 + 576 - hb1 * 576
    rb2 = rb1 + hb2 * 288
    sb2 = rb1 + 288 - hb2 * 288
    rk = ra2 + zlo * (rb2 - ra2)
    rs = rb2 + zlo * (ra2 - rb2)

    def rows(ref, a, r, n):
        return ref.at[a, pl.ds(mo(r), n)]

    def add(a, r, n, land, step):
        def one(i, _):
            at = pl.ds(mo(r + i * step), step)
            g[a, at] = (g[a, at].astype(F32) + land[pl.ds(mo(i * step), step)].astype(F32)).astype(BF16)
            return 0

        lax.fori_loop(0, n // step, one, 0)

    def reduce(a):
        c0 = send(rows(g, a, other, 2304), lc.at[a], core_dev)
        yield
        c0.wait_recv()
        add(a, base, 2304, lc.at[a], 288)
        c1 = send(rows(g, a, sa1, 576), l1.at[a, 0], xa_dev)
        c2 = send(rows(g, a, sb1, 576), l1.at[a, 1], xb_dev)
        yield
        c1.wait_recv()
        add(a, ra1, 576, l1.at[a, 0], 288)
        c3 = send(rows(g, a, sa2, 288), l2.at[a, 0], xb_dev)
        c2.wait_recv()
        add(a, rb1, 576, l1.at[a, 1], 288)
        c4 = send(rows(g, a, sb2, 288), l2.at[a, 1], xa_dev)
        yield
        c3.wait_recv()
        add(a, ra2, 288, l2.at[a, 0], 288)
        c4.wait_recv()
        add(a, rb2, 288, l2.at[a, 1], 288)
        c5 = send(rows(g, a, rs, 288), l3.at[a], zlo_dev)
        yield
        c5.wait_recv()
        fo[a, pl.ds(mo(rk), 288)] = (
            g[a, pl.ds(mo(rk), 288)].astype(F32) + l3[a].astype(F32)
        ).astype(BF16)
        c6 = send(rows(fo, a, rk, 288), rows(fo, a, rk, 288), zlo_dev)
        yield
        c6.wait_recv()
        c7 = send(rows(fo, a, ra2, 288), rows(fo, a, ra2, 288), xb_dev)
        c8 = send(rows(fo, a, rb2, 288), rows(fo, a, rb2, 288), xa_dev)
        yield
        c7.wait_recv()
        c9 = send(rows(fo, a, ra1, 576), rows(fo, a, ra1, 576), xa_dev)
        c8.wait_recv()
        c10 = send(rows(fo, a, rb1, 576), rows(fo, a, rb1, 576), xb_dev)
        yield
        c9.wait_recv()
        c10.wait_recv()
        c11 = send(rows(fo, a, base, 2304), rows(fo, a, base, 2304), core_dev)
        yield
        c11.wait_recv()
        out = pltpu.make_async_copy(fo.at[a], (outg_o, ing_o)[a], lsem.at[3 + a])
        out.start()
        yield
        out.wait()

    def step(task):
        next(task, None)

    pre = by_panel(0)
    cdf = 0.5 * (1.0 + lax.erf(pre * 0.7071067811865476))
    hd[0, :NPAN] = (pre * cdf).astype(BF16).reshape(NPAN, 128, 128)
    slope = cdf + pre * jnp.exp(-0.5 * pre * pre) * 0.3989422804014327
    d_pre = lax.dot_general(
        wd[1], x[1].reshape(128, D), nt, preferred_element_type=F32
    )
    hd[1, :NPAN] = (d_pre * slope).astype(BF16).reshape(NPAN, 128, 128)

    blocks(1)
    grads(0, 1, 1, 0)
    red0, red1 = reduce(0), reduce(1)
    step(red0)
    blocks(0)
    grads(1, 0, 0, 1)
    step(red0)
    step(red1)
    partial(0, 0, 1)
    sc0, sc1 = scatter(0), scatter(1)
    step(sc0)
    step(red0)
    step(red1)
    partial(1, 1, 0)
    step(sc1)
    tasks = [red0, sc0, red1, sc1]
    while tasks:
        for task in list(tasks):
            if next(task, tasks) is tasks:
                tasks.remove(task)
    for c in started:
        c.wait_send()


def slot_table(in_rows, in_cols, out_rows, out_cols):
    rows, cols = jnp.stack([in_rows, out_rows]), jnp.stack([in_cols, out_cols])
    live = rows >= 0
    panel = jnp.where(live, rows % NPAN, NPAN)
    col = jnp.where(live, cols, 0)
    pair = jnp.arange(NPAN * NCOL, dtype=jnp.int32)
    slot = jnp.arange(CAP, dtype=jnp.int32)
    hit = (panel * NCOL + col)[:, :, None] == pair[None, None, :]
    where = jnp.min(jnp.where(hit, slot[None, :, None], CAP), axis=1)
    return jnp.concatenate([where, panel, col], axis=1)


def local(tokens, cotangent, w_in, w_out, in_rows, in_cols, out_rows, out_cols):
    vmem = pl.BlockSpec(memory_space=pltpu.VMEM)
    smem = pl.BlockSpec(memory_space=pltpu.SMEM)
    hbm = pl.BlockSpec(memory_space=pl.ANY)
    rows = tokens.shape[0]
    mixed, igrad, ing, outg = pl.pallas_call(
        kernel,
        out_shape=(
            jax.ShapeDtypeStruct((rows, D), BF16),
            jax.ShapeDtypeStruct((rows, D), BF16),
            jax.ShapeDtypeStruct((CAP * 128, 128), BF16),
            jax.ShapeDtypeStruct((CAP * 128, 128), BF16),
        ),
        in_specs=[vmem, vmem, hbm, hbm, smem],
        out_specs=(vmem, vmem, hbm, hbm),
        scratch_shapes=[
            pltpu.VMEM((2, NY, 16, D), BF16),
            pltpu.VMEM((2, NZ, 16, 1024), BF16),
            pltpu.VMEM((2, 16, 1024), F32),
            pltpu.VMEM((2, 16, D), F32),
            pltpu.VMEM((2, CAP + 1, 128, 128), BF16),
            pltpu.VMEM((2, 512, D), BF16),
            pltpu.VMEM((2, NCOL, 128, 128), BF16),
            pltpu.VMEM((2, NPAN + 1, 128, 128), BF16),
            pltpu.VMEM((2, NY, 16, D), BF16),
            pltpu.VMEM((2, 4, 16, D), BF16),
            pltpu.VMEM((2, 4, 16, D), BF16),
            pltpu.VMEM((2, NZ, 16, 1024), BF16),
            pltpu.VMEM((2, NZ, 16, 1024), BF16),
            pltpu.VMEM((2, 4608, 128), BF16),
            pltpu.VMEM((2, 4608, 128), BF16),
            pltpu.VMEM((2, 2304, 128), BF16),
            pltpu.VMEM((2, 2, 576, 128), BF16),
            pltpu.VMEM((2, 2, 288, 128), BF16),
            pltpu.VMEM((2, 288, 128), BF16),
            pltpu.SemaphoreType.DMA((SEMS,)),
            pltpu.SemaphoreType.DMA((SEMS,)),
            pltpu.SemaphoreType.DMA((5,)),
        ],
        compiler_params=pltpu.CompilerParams(
            collective_id=0, has_side_effects=True, vmem_limit_bytes=56 * 2**20
        ),
    )(tokens, cotangent, w_in, w_out, slot_table(in_rows, in_cols, out_rows, out_cols))
    return mixed, igrad, ing.reshape(CAP, 128, 128), outg.reshape(CAP, 128, 128)


def solution(mesh):
    placed = (
        P(("dp", "fsdp"), None),
        P(("dp", "fsdp"), None),
        P("fsdp", None, None),
        P("fsdp", None, None),
        P("fsdp"),
        P("fsdp"),
        P("fsdp"),
        P("fsdp"),
    )
    return jax.shard_map(
        local,
        mesh=mesh,
        in_specs=placed,
        out_specs=(
            P(("dp", "fsdp"), None),
            P(("dp", "fsdp"), None),
            P("fsdp", None, None),
            P("fsdp", None, None),
        ),
        check_vma=False,
    )
```

```python
import jax
import jax.numpy as jnp
from jax import lax
from jax.experimental import pallas as pl
from jax.experimental.pallas import tpu as pltpu
from jax.sharding import PartitionSpec as P

MESH = pl.DeviceIdType.MESH
F32 = jnp.float32
BF16 = jnp.bfloat16

NY, NZ = 8, 4
CAP = 36
NCOL = 32
NPAN = 4
D = 4096
SEMS = 128


def mo(v, m=16):
    return pl.multiple_of(v, m)


def kernel(
    tok, cot, w_in, w_out, pair_slot, slot_pair,
    mixed_o, igrad_o, ing_o, outg_o,
    own, xg, x, t1, t2, ws, wd, xb, hd, prt, rland, lland, zs, zl, g, lc, l1, l2, l3,
    ssem, rsem, lsem,
):
    dp, fs = lax.axis_index("dp"), lax.axis_index("fsdp")
    y, zh = fs // NZ, fs % NZ
    px, zlo, core = dp // 4, (dp // 2) % 2, dp % 2

    def dev(d=dp, f=fs):
        return (d, f)

    z_peers = [(zh + d) % NZ for d in (1, 2, 3)]
    z_devs = [dev(f=y * NZ + j) for j in z_peers]
    right = dev(f=((y + 1) % NY) * NZ + zh)
    left = dev(f=((y + NY - 1) % NY) * NZ + zh)
    core_dev = dev(d=dp + 1 - 2 * core)
    xpa = px + 1 - 2 * (px % 2)
    xpb = (px + 2 * (px % 2) + 3) % 4
    xa_dev = dev(d=xpa * 4 + dp % 4)
    xb_dev = dev(d=xpb * 4 + dp % 4)
    zlo_dev = dev(d=dp + 2 - 4 * zlo)
    everyone = [*z_devs, right, left, core_dev, xa_dev, xb_dev, zlo_dev]

    used = [0]
    started = []

    def send(src, dst, to):
        i = used[0]
        used[0] += 1
        c = pltpu.make_async_remote_copy(
            src, dst, ssem.at[i], rsem.at[i], device_id=to, device_id_type=MESH
        )
        c.start()
        started.append(c)
        return c

    barrier = pltpu.get_barrier_semaphore()
    for to in everyone:
        pl.semaphore_signal(barrier, inc=1, device_id=to, device_id_type=MESH)

    fetch = [
        pltpu.make_async_copy(src, own.at[a], lsem.at[2 + a])
        for a, src in enumerate((tok, cot))
    ]
    weights = [
        pltpu.make_async_copy(w, ws.at[a, pl.ds(0, CAP)], lsem.at[a])
        for a, w in enumerate((w_in, w_out))
    ]
    for c in fetch + weights:
        c.start()

    for a in range(2):
        fetch[a].wait()
        for k in range(4):
            t1[a, 4 * k : 4 * k + 4, :] = own[a, :, 1024 * k : 1024 * (k + 1)].astype(F32)
        xg[a, y, 0] = t1[a].astype(BF16)

    pl.semaphore_wait(barrier, len(everyone))

    zsend = [
        [send(xg.at[a, y, 0], xg.at[a, y, NZ - d], to) for d, to in zip((1, 2, 3), z_devs)]
        for a in range(2)
    ]
    for a in range(2):
        ws[a, CAP] = jnp.zeros((128, 128), BF16)
        hd[a, NPAN] = jnp.zeros((128, 128), BF16)

    def unfold(a, b):
        for d in range(NZ):
            t1[a] = xg[a, b, d].astype(F32)
            for k in range(4):
                t2[a, 4 * d : 4 * d + 4, 1024 * k : 1024 * (k + 1)] = t1[a, 4 * k : 4 * k + 4, :]
        x[a, b] = t2[a].astype(BF16)

    rights, lefts = (4, 3), (3, 4)
    chains = {}

    def hop(a, grp, k):
        part = (pl.ds(0, 1), pl.ds(1, 3))[grp]
        for way, to, n, back in (
            (0, right, rights[a ^ grp], NY - 1),
            (1, left, lefts[a ^ grp], 1),
        ):
            chain = chains.setdefault((a, grp, way), [])
            if k < n:
                if k:
                    chain[k - 1].wait_recv()
                ref = xg.at[a, (y + back * k) % NY, part]
                chain.append(send(ref, ref, to))

    def arrive(a, k):
        for grp in range(2):
            for way in range(2):
                chain = chains[(a, grp, way)]
                if k == len(chain):
                    chain[k - 1].wait_recv()
        unfold(a, (y + NY - k) % NY)
        if 2 * k != NY and k:
            unfold(a, (y + k) % NY)

    def dense(a):
        if a == 0:
            for w in weights:
                w.wait()

        def one(c, _):
            for p in range(NPAN):
                slot = pair_slot[a, p * NCOL + c]
                wd[a, pl.ds(p * 128, 128), pl.ds(mo(c * 128, 128), 128)] = ws[a, slot]
            return 0

        lax.fori_loop(0, NCOL, one, 0)

    hop(0, 0, 0)
    hop(1, 0, 0)
    hop(0, 0, 1)
    hop(1, 0, 1)
    for a in range(2):
        for c in zsend[a]:
            c.wait_recv()
        hop(a, 1, 0)
    hop(0, 0, 2)
    hop(1, 0, 2)
    dense(0)
    hop(0, 1, 1)
    hop(1, 1, 1)
    hop(0, 0, 3)
    hop(1, 0, 3)
    dense(1)
    hop(0, 1, 2)
    hop(1, 1, 2)
    arrive(0, 0)
    arrive(1, 0)
    arrive(0, 1)
    arrive(1, 1)
    hop(0, 1, 3)
    hop(1, 1, 3)
    for k in (2, 3, 4):
        arrive(0, k)
        arrive(1, k)

    nt = (((1,), (1,)), ((), ()))

    def by_panel(a):
        return lax.dot_general(wd[a], x[a].reshape(128, D), nt, preferred_element_type=F32)

    def blocks(a):
        def one(c, _):
            xb[a, c] = x[a, :, :, pl.ds(mo(c * 128, 128), 128)].reshape(128, 128)
            return 0

        lax.fori_loop(0, NCOL, one, 0)

    def grads(dst, half):
        a = 1 - dst

        def one(i, _):
            s = i + half * (CAP // 2)
            pair = slot_pair[a, s]
            blk = jnp.dot(hd[dst, pair // NCOL], xb[a, pair % NCOL], preferred_element_type=F32)
            g[dst, pl.ds(mo(s * 128, 128), 128), :] = blk.astype(BF16)
            return 0

        lax.fori_loop(0, CAP // 2, one, 0, unroll=6)

    def partial(dst, side, a):
        acts = hd[side, :NPAN].reshape(512, 128).astype(F32).T.astype(BF16)

        def one(n, _):
            cols = pl.ds(mo(n * 512, 512), 512)
            part = jnp.dot(acts, wd[a, :, cols], preferred_element_type=F32)
            prt[dst, :, :, cols] = part.astype(BF16).reshape(NY, 16, 512)
            return 0

        lax.fori_loop(0, D // 512, one, 0)

    def scatter(a):
        nr, nl = rights[a], lefts[a]
        rc = [send(prt.at[a, (y + nr) % NY], rland.at[a, 0], right)]
        lc_ = [send(prt.at[a, (y + NY - nl) % NY], lland.at[a, 0], left)]
        for k in range(1, 4):
            for chain, land, n, to, sign in (
                (rc, rland, nr, right, 1),
                (lc_, lland, nl, left, NY - 1),
            ):
                if k >= n:
                    continue
                yield
                chain[k - 1].wait_recv()
                own = prt[a, (y + sign * (n - k)) % NY].astype(F32)
                land[a, k - 1] = (own + land[a, k - 1].astype(F32)).astype(BF16)
                chain.append(send(land.at[a, k - 1], land.at[a, k], to))
        yield
        rc[-1].wait_recv()
        lc_[-1].wait_recv()
        t2[a] = (
            prt[a, y].astype(F32)
            + rland[a, nr - 1].astype(F32)
            + lland[a, nl - 1].astype(F32)
        )
        for j in range(NZ):
            for k in range(4):
                t1[a, 4 * k : 4 * k + 4, :] = t2[a, 4 * j : 4 * j + 4, 1024 * k : 1024 * (k + 1)]
            zs[a, j] = t1[a].astype(BF16)
        out = [
            send(zs.at[a, d], zl.at[a, NZ - d], to) for d, to in zip((1, 2, 3), z_devs)
        ]
        yield
        for c in out:
            c.wait_recv()
        total = zs[a, 0].astype(F32)
        for d in (1, 2, 3):
            total = total + zl[a, d].astype(F32)
        t1[a] = total
        dst = (mixed_o, igrad_o)[a]
        for k in range(4):
            dst[:, 1024 * k : 1024 * (k + 1)] = t1[a, 4 * k : 4 * k + 4, :].astype(BF16)

    ha1, ha2 = ((px + 1) // 2) % 2, px // 2
    hb1, hb2 = px // 2, px % 2
    half_rows = CAP * 64
    n1, n2, n3, n4 = (half_rows // m for m in (2, 4, 8, 16))

    def rows(ref, r, n):
        return ref.at[pl.ds(mo(r), n)]

    def reduce(a, half):
        i = 2 * a + half
        ga, fo = g.at[a], (outg_o, ing_o)[a]
        base = half * half_rows + core * n1
        other = half * half_rows + n1 - core * n1
        ra1 = base + ha1 * n3
        sa1 = base + n3 - ha1 * n3
        ra2 = ra1 + ha2 * n4
        sa2 = ra1 + n4 - ha2 * n4
        rb1 = base + n2 + hb1 * n3
        sb1 = base + n2 + n3 - hb1 * n3
        rb2 = rb1 + hb2 * n4
        sb2 = rb1 + n4 - hb2 * n4
        rk = ra2 + zlo * (rb2 - ra2)
        rs = rb2 + zlo * (ra2 - rb2)

        def add(r, n, land):
            def one(c, _):
                at = pl.ds(mo(r + c * n4), n4)
                got = land[pl.ds(mo(c * n4), n4)].astype(F32)
                g[a, at] = (g[a, at].astype(F32) + got).astype(BF16)
                return 0

            lax.fori_loop(0, n // n4, one, 0)

        c0 = send(rows(ga, other, n1), lc.at[i], core_dev)
        yield
        c0.wait_recv()
        add(base, n1, lc.at[i])
        c1 = send(rows(ga, sa1, n3), l1.at[i, 0], xa_dev)
        c2 = send(rows(ga, sb1, n3), l1.at[i, 1], xb_dev)
        yield
        c1.wait_recv()
        add(ra1, n3, l1.at[i, 0])
        c3 = send(rows(ga, sa2, n4), l2.at[i, 0], xb_dev)
        c2.wait_recv()
        add(rb1, n3, l1.at[i, 1])
        c4 = send(rows(ga, sb2, n4), l2.at[i, 1], xa_dev)
        yield
        c3.wait_recv()
        add(ra2, n4, l2.at[i, 0])
        c4.wait_recv()
        add(rb2, n4, l2.at[i, 1])
        c5 = send(rows(ga, rs, n4), l3.at[i], zlo_dev)
        yield
        c5.wait_recv()
        fo[pl.ds(mo(rk), n4)] = (
            g[a, pl.ds(mo(rk), n4)].astype(F32) + l3[i].astype(F32)
        ).astype(BF16)
        c6 = send(rows(fo, rk, n4), rows(fo, rk, n4), zlo_dev)
        yield
        c6.wait_recv()
        c7 = send(rows(fo, ra2, n4), rows(fo, ra2, n4), xb_dev)
        c8 = send(rows(fo, rb2, n4), rows(fo, rb2, n4), xa_dev)
        yield
        c7.wait_recv()
        c9 = send(rows(fo, ra1, n3), rows(fo, ra1, n3), xa_dev)
        c8.wait_recv()
        c10 = send(rows(fo, rb1, n3), rows(fo, rb1, n3), xb_dev)
        yield
        c9.wait_recv()
        c10.wait_recv()
        c11 = send(rows(fo, base, n1), rows(fo, base, n1), core_dev)
        yield
        c11.wait_recv()

    def step(task):
        next(task, None)

    pre = by_panel(0)
    cdf = 0.5 * (1.0 + lax.erf(pre * 0.7071067811865476))
    hd[0, :NPAN] = (pre * cdf).astype(BF16).reshape(NPAN, 128, 128)
    slope = cdf + pre * jnp.exp(-0.5 * pre * pre) * 0.3989422804014327
    d_pre = lax.dot_general(
        wd[1], x[1].reshape(128, D), nt, preferred_element_type=F32
    )
    hd[1, :NPAN] = (d_pre * slope).astype(BF16).reshape(NPAN, 128, 128)

    red = [reduce(i // 2, i % 2) for i in range(4)]
    sc0, sc1 = scatter(0), scatter(1)
    blocks(1)
    grads(0, 0)
    step(red[0])
    grads(0, 1)
    step(red[1])
    blocks(0)
    step(red[0])
    grads(1, 0)
    step(red[2])
    step(red[1])
    grads(1, 1)
    step(red[3])
    step(red[0])
    partial(0, 0, 1)
    step(sc0)
    for i in (1, 2, 3, 0):
        step(red[i])
    partial(1, 1, 0)
    step(sc1)
    tasks = [red[1], red[2], sc0, red[3], red[0], sc1]
    while tasks:
        for task in list(tasks):
            if next(task, tasks) is tasks:
                tasks.remove(task)
    for c in started:
        c.wait_send()


def copy_out(*refs):
    n = (len(refs) - 1) // 2
    copies = [pltpu.make_async_copy(refs[i], refs[n + i], refs[-1].at[i]) for i in range(n)]
    for c in copies:
        c.start()
    for c in copies:
        c.wait()


def slot_tables(in_rows, in_cols, out_rows, out_cols):
    rows, cols = jnp.stack([in_rows, out_rows]), jnp.stack([in_cols, out_cols])
    pair = jnp.where(rows >= 0, (rows % NPAN) * NCOL + cols, NPAN * NCOL)
    slot = jnp.arange(CAP, dtype=jnp.int32)
    hit = pair[:, :, None] == jnp.arange(NPAN * NCOL, dtype=jnp.int32)[None, None, :]
    return pair, jnp.min(jnp.where(hit, slot[None, :, None], CAP), axis=1)


def local(tokens, cotangent, w_in, w_out, in_rows, in_cols, out_rows, out_cols):
    smem = pl.BlockSpec(memory_space=pltpu.SMEM)
    hbm = pl.BlockSpec(memory_space=pl.ANY)
    vmem = pl.BlockSpec(memory_space=pltpu.VMEM)
    rows = tokens.shape[0]
    shapes = [(rows, D), (rows, D), (CAP * 128, 128), (CAP * 128, 128)]
    slot_pair, pair_slot = slot_tables(in_rows, in_cols, out_rows, out_cols)
    half = CAP * 64
    results = pl.pallas_call(
        kernel,
        out_shape=tuple(pltpu.VMEM(s, BF16) for s in shapes),
        in_specs=[hbm, hbm, hbm, hbm, smem, smem],
        out_specs=(vmem,) * 4,
        scratch_shapes=[
            pltpu.VMEM((2, rows, D), BF16),
            pltpu.VMEM((2, NY, NZ, 16, 1024), BF16),
            pltpu.VMEM((2, NY, 16, D), BF16),
            pltpu.VMEM((2, 16, 1024), F32),
            pltpu.VMEM((2, 16, D), F32),
            pltpu.VMEM((2, CAP + 1, 128, 128), BF16),
            pltpu.VMEM((2, 512, D), BF16),
            pltpu.VMEM((2, NCOL, 128, 128), BF16),
            pltpu.VMEM((2, NPAN + 1, 128, 128), BF16),
            pltpu.VMEM((2, NY, 16, D), BF16),
            pltpu.VMEM((2, 4, 16, D), BF16),
            pltpu.VMEM((2, 4, 16, D), BF16),
            pltpu.VMEM((2, NZ, 16, 1024), BF16),
            pltpu.VMEM((2, NZ, 16, 1024), BF16),
            pltpu.VMEM((2, CAP * 128, 128), BF16),
            pltpu.VMEM((4, half // 2, 128), BF16),
            pltpu.VMEM((4, 2, half // 8, 128), BF16),
            pltpu.VMEM((4, 2, half // 16, 128), BF16),
            pltpu.VMEM((4, half // 16, 128), BF16),
            pltpu.SemaphoreType.DMA((SEMS,)),
            pltpu.SemaphoreType.DMA((SEMS,)),
            pltpu.SemaphoreType.DMA((4,)),
        ],
        compiler_params=pltpu.CompilerParams(
            collective_id=0, has_side_effects=True, vmem_limit_bytes=52 * 2**20
        ),
    )(tokens, cotangent, w_in, w_out, pair_slot, slot_pair)
    mixed, igrad, ing, outg = pl.pallas_call(
        copy_out,
        out_shape=tuple(jax.ShapeDtypeStruct(s, BF16) for s in shapes),
        in_specs=[vmem] * 4,
        out_specs=(hbm,) * 4,
        scratch_shapes=[pltpu.SemaphoreType.DMA((4,))],
        compiler_params=pltpu.CompilerParams(has_side_effects=True),
    )(*(pltpu.with_memory_space_constraint(r, pltpu.VMEM) for r in results))
    return mixed, igrad, ing.reshape(CAP, 128, 128), outg.reshape(CAP, 128, 128)


def solution(mesh):
    placed = (
        P(("dp", "fsdp"), None),
        P(("dp", "fsdp"), None),
        P("fsdp", None, None),
        P("fsdp", None, None),
        P("fsdp"),
        P("fsdp"),
        P("fsdp"),
        P("fsdp"),
    )
    return jax.shard_map(
        local,
        mesh=mesh,
        in_specs=placed,
        out_specs=(
            P(("dp", "fsdp"), None),
            P(("dp", "fsdp"), None),
            P("fsdp", None, None),
            P("fsdp", None, None),
        ),
        check_vma=False,
    )
```

```python
import jax
import jax.numpy as jnp
from jax import lax
from jax.experimental import pallas as pl
from jax.experimental.pallas import tpu as pltpu
from jax.sharding import PartitionSpec as P

MESH = pl.DeviceIdType.MESH
F32 = jnp.float32
BF16 = jnp.bfloat16

NY, NZ = 8, 4
CAP = 36
NCOL = 32
NPAN = 4
D = 4096
SEMS = 128


def mo(v, m=16):
    return pl.multiple_of(v, m)


def kernel(
    tok, cot, w_in, w_out, pair_slot, slot_pair,
    mixed_o, igrad_o, ing_o, outg_o,
    own, xg, x, t1, t2, t3, t4, ws, wd, xb, hd, acts, prt, rland, lland, zs, zl, g, lc, l1, l2, l3, slope_ref,
    ssem, rsem, lsem,
):
    dp, fs = lax.axis_index("dp"), lax.axis_index("fsdp")
    y, zh = fs // NZ, fs % NZ
    px, zlo, core = dp // 4, (dp // 2) % 2, dp % 2

    def dev(d=dp, f=fs):
        return (d, f)

    z_peers = [(zh + d) % NZ for d in (1, 2, 3)]
    z_devs = [dev(f=y * NZ + j) for j in z_peers]
    right = dev(f=((y + 1) % NY) * NZ + zh)
    left = dev(f=((y + NY - 1) % NY) * NZ + zh)
    core_dev = dev(d=dp + 1 - 2 * core)
    xpa = px + 1 - 2 * (px % 2)
    xpb = (px + 2 * (px % 2) + 3) % 4
    xa_dev = dev(d=xpa * 4 + dp % 4)
    xb_dev = dev(d=xpb * 4 + dp % 4)
    zlo_dev = dev(d=dp + 2 - 4 * zlo)
    everyone = [*z_devs, right, left, core_dev, xa_dev, xb_dev, zlo_dev]

    used = [0]
    started = []

    def send(src, dst, to):
        i = used[0]
        used[0] += 1
        c = pltpu.make_async_remote_copy(
            src, dst, ssem.at[i], rsem.at[i], device_id=to, device_id_type=MESH
        )
        c.start()
        started.append(c)
        return c

    barrier = pltpu.get_barrier_semaphore()
    for to in everyone:
        pl.semaphore_signal(barrier, inc=1, device_id=to, device_id_type=MESH)

    fetch = [
        pltpu.make_async_copy(src, own.at[a], lsem.at[2 + a])
        for a, src in enumerate((tok, cot))
    ]
    weights = [
        pltpu.make_async_copy(w, ws.at[a, pl.ds(0, CAP)], lsem.at[a])
        for a, w in enumerate((w_in, w_out))
    ]
    for c in fetch + weights:
        c.start()

    for a in range(2):
        fetch[a].wait()
        for k in range(4):
            t1[a, 4 * k : 4 * k + 4, :] = own[a, :, 1024 * k : 1024 * (k + 1)].astype(F32)
        xg[a, y, 0] = t1[a].astype(BF16)

    pl.semaphore_wait(barrier, len(everyone))

    zsend = [
        [send(xg.at[a, y, 0], xg.at[a, y, NZ - d], to) for d, to in zip((1, 2, 3), z_devs)]
        for a in range(2)
    ]
    for a in range(2):
        ws[a, CAP] = jnp.zeros((128, 128), BF16)
        hd[a, NPAN] = jnp.zeros((128, 128), BF16)

    def unfold(a, b):
        for d in range(NZ):
            t1[a] = xg[a, b, d].astype(F32)
            for k in range(4):
                t2[a, 4 * d : 4 * d + 4, 1024 * k : 1024 * (k + 1)] = t1[a, 4 * k : 4 * k + 4, :]
        rows = t2[a].astype(BF16)
        x[a, b] = rows
        for c in range(NCOL):
            xb[a, c, pl.ds(mo(b * 16), 16), :] = rows[:, 128 * c : 128 * (c + 1)]

    rights, lefts = (4, 3), (3, 4)
    chains = {}

    def hop(a, grp, k):
        part = (pl.ds(0, 1), pl.ds(1, 3))[grp]
        for way, to, n, back in (
            (0, right, rights[a ^ grp], NY - 1),
            (1, left, lefts[a ^ grp], 1),
        ):
            chain = chains.setdefault((a, grp, way), [])
            if k < n:
                if k:
                    chain[k - 1].wait_recv()
                ref = xg.at[a, (y + back * k) % NY, part]
                chain.append(send(ref, ref, to))

    def arrive(a, k):
        for grp in range(2):
            for way in range(2):
                chain = chains[(a, grp, way)]
                if k == len(chain):
                    chain[k - 1].wait_recv()
        unfold(a, (y + NY - k) % NY)
        if 2 * k != NY and k:
            unfold(a, (y + k) % NY)

    def dense(a):
        if a == 0:
            for w in weights:
                w.wait()

        def one(c, _):
            for p in range(NPAN):
                slot = pair_slot[a, p * NCOL + c]
                wd[a, pl.ds(p * 128, 128), pl.ds(mo(c * 128, 128), 128)] = ws[a, slot]
            return 0

        lax.fori_loop(0, NCOL, one, 0)

    hop(0, 0, 0)
    hop(1, 0, 0)
    hop(0, 0, 1)
    hop(1, 0, 1)
    for a in range(2):
        for c in zsend[a]:
            c.wait_recv()
        hop(a, 1, 0)
    hop(0, 0, 2)
    hop(1, 0, 2)
    dense(0)
    hop(0, 1, 1)
    hop(1, 1, 1)
    hop(0, 0, 3)
    hop(1, 0, 3)
    dense(1)
    hop(0, 1, 2)
    hop(1, 1, 2)
    arrive(0, 0)
    arrive(1, 0)
    arrive(0, 1)
    arrive(1, 1)
    arrive(0, 2)
    arrive(1, 2)
    hop(0, 1, 3)
    hop(1, 1, 3)
    arrive(0, 3)
    arrive(0, 4)

    nt = (((1,), (1,)), ((), ()))

    def by_panel(a):
        return lax.dot_general(wd[a], x[a].reshape(128, D), nt, preferred_element_type=F32)

    def grads(dst, half):
        a = 1 - dst

        def one(i, _):
            s = i + half * (CAP // 2)
            pair = slot_pair[a, s]
            blk = jnp.dot(hd[dst, pair // NCOL], xb[a, pair % NCOL], preferred_element_type=F32)
            g[dst, pl.ds(mo(s * 128, 128), 128), :] = blk.astype(BF16)
            return 0

        lax.fori_loop(0, CAP // 2, one, 0, unroll=6)

    half_d = D // 2

    def by_token(side):
        acts[side] = hd[side, :NPAN].reshape(512, 128).astype(F32).T.astype(BF16)

    def partial(a, half):
        def one(n, _):
            cols = pl.ds(mo(half * half_d + n * 512, 512), 512)
            part = jnp.dot(acts[a], wd[1 - a, :, cols], preferred_element_type=F32)
            prt[a, half, :, :, pl.ds(mo(n * 512, 512), 512)] = part.astype(BF16).reshape(NY, 16, 512)
            return 0

        lax.fori_loop(0, half_d // 512, one, 0)

    def scatter(a, half):
        own_part, from_left, from_right = prt.at[a, half], rland.at[a, half], lland.at[a, half]
        send_z, land_z = zs.at[a, half], zl.at[a, half]
        nr, nl = rights[a ^ half], lefts[a ^ half]
        ways = (
            ([send(own_part.at[(y + nr) % NY], from_left.at[0], right)], from_left, nr, right, 1),
            ([send(own_part.at[(y + NY - nl) % NY], from_right.at[0], left)], from_right, nl, left, NY - 1),
        )
        for k in range(1, 4):
            yield
            for chain, land, n, to, sign in ways:
                if k < n:
                    chain[k - 1].wait_recv()
                    mine = own_part[(y + sign * (n - k)) % NY].astype(F32)
                    land[k - 1] = (mine + land[k - 1].astype(F32)).astype(BF16)
                    chain.append(send(land.at[k - 1], land.at[k], to))
        yield
        for chain, _, _, _, _ in ways:
            chain[-1].wait_recv()
        t3[...] = (
            own_part[y].astype(F32)
            + from_left[nr - 1].astype(F32)
            + from_right[nl - 1].astype(F32)
        )
        w = half_d // 4
        for d in range(NZ):
            for k in range(4):
                t4[d, 4 * k : 4 * k + 4, :] = t3[4 * d : 4 * d + 4, w * k : w * (k + 1)]
            send_z[d] = t4[d].astype(BF16)
        out = [
            send(send_z.at[d], land_z.at[NZ - d], to) for d, to in zip((1, 2, 3), z_devs)
        ]
        yield
        for c in out:
            c.wait_recv()
        total = send_z[0].astype(F32)
        for d in (1, 2, 3):
            total = total + land_z[d].astype(F32)
        t4[0] = total
        dst = (mixed_o, igrad_o)[a]
        for k in range(4):
            at = half * half_d + w * k
            dst[:, at : at + w] = t4[0, 4 * k : 4 * k + 4, :].astype(BF16)

    ha1, ha2 = ((px + 1) // 2) % 2, px // 2
    hb1, hb2 = px // 2, px % 2
    half_rows = CAP * 64
    n1, n2, n3, n4 = (half_rows // m for m in (2, 4, 8, 16))

    def rows(ref, r, n):
        return ref.at[pl.ds(mo(r), n)]

    def reduce(a, half):
        i = 2 * a + half
        ga, fo = g.at[a], (outg_o, ing_o)[a]
        base = half * half_rows + core * n1
        other = half * half_rows + n1 - core * n1
        ra1 = base + ha1 * n3
        sa1 = base + n3 - ha1 * n3
        ra2 = ra1 + ha2 * n4
        sa2 = ra1 + n4 - ha2 * n4
        rb1 = base + n2 + hb1 * n3
        sb1 = base + n2 + n3 - hb1 * n3
        rb2 = rb1 + hb2 * n4
        sb2 = rb1 + n4 - hb2 * n4

        def add(r, n, land):
            def one(c, _):
                at = pl.ds(mo(r + c * n4), n4)
                got = land[pl.ds(mo(c * n4), n4)].astype(F32)
                g[a, at] = (g[a, at].astype(F32) + got).astype(BF16)
                return 0

            lax.fori_loop(0, n // n4, one, 0)

        c0 = send(rows(ga, other, n1), lc.at[i], core_dev)
        yield
        c0.wait_recv()
        add(base, n1, lc.at[i])
        c1 = send(rows(ga, sa1, n3), l1.at[i, 0], xa_dev)
        c2 = send(rows(ga, sb1, n3), l1.at[i, 1], xb_dev)
        yield
        c1.wait_recv()
        add(ra1, n3, l1.at[i, 0])
        c3 = send(rows(ga, sa2, n4), l2.at[i, 0], xb_dev)
        c2.wait_recv()
        add(rb1, n3, l1.at[i, 1])
        c4 = send(rows(ga, sb2, n4), l2.at[i, 1], xa_dev)
        yield
        c3.wait_recv()
        add(ra2, n4, l2.at[i, 0])
        c4.wait_recv()
        add(rb2, n4, l2.at[i, 1])
        c5 = send(rows(ga, ra2, n4), l3.at[i, 0], zlo_dev)
        c6 = send(rows(ga, rb2, n4), l3.at[i, 1], zlo_dev)
        yield
        for c, r, land in ((c5, ra2, l3.at[i, 0]), (c6, rb2, l3.at[i, 1])):
            c.wait_recv()
            both = g[a, pl.ds(mo(r), n4)].astype(F32) + land[...].astype(F32)
            fo[pl.ds(mo(r), n4)] = both.astype(BF16)
        c7 = send(rows(fo, ra2, n4), rows(fo, ra2, n4), xb_dev)
        c8 = send(rows(fo, rb2, n4), rows(fo, rb2, n4), xa_dev)
        yield
        c7.wait_recv()
        c9 = send(rows(fo, ra1, n3), rows(fo, ra1, n3), xa_dev)
        c8.wait_recv()
        c10 = send(rows(fo, rb1, n3), rows(fo, rb1, n3), xb_dev)
        yield
        c9.wait_recv()
        c10.wait_recv()
        c11 = send(rows(fo, base, n1), rows(fo, base, n1), core_dev)
        yield
        c11.wait_recv()

    def step(task):
        next(task, None)

    red = [reduce(i // 2, i % 2) for i in range(4)]
    sca = [[scatter(a, half) for half in range(2)] for a in range(2)]

    pre = by_panel(0)
    cdf = 0.5 * (1.0 + lax.erf(pre * 0.7071067811865476))
    hd[0, :NPAN] = (pre * cdf).astype(BF16).reshape(NPAN, 128, 128)
    slope_ref[...] = cdf + pre * jnp.exp(-0.5 * pre * pre) * 0.3989422804014327
    by_token(0)
    for half in range(2):
        partial(0, half)
        step(sca[0][half])
    arrive(1, 3)
    arrive(1, 4)
    grads(0, 0)
    step(red[0])
    grads(0, 1)
    step(red[1])
    step(sca[0][0])
    d_pre = by_panel(1)
    hd[1, :NPAN] = (d_pre * slope_ref[...]).astype(BF16).reshape(NPAN, 128, 128)
    step(red[0])
    step(sca[0][1])
    grads(1, 0)
    step(red[2])
    step(red[1])
    grads(1, 1)
    step(red[3])
    by_token(1)
    step(red[0])
    partial(1, 0)
    step(sca[1][0])
    step(sca[0][0])
    step(red[2])
    partial(1, 1)
    step(sca[1][1])
    step(sca[0][1])
    step(red[1])
    step(red[3])
    tasks = [red[0], sca[1][0], red[2], sca[0][0], red[1], sca[1][1], red[3], sca[0][1]]
    while tasks:
        for task in list(tasks):
            if next(task, tasks) is tasks:
                tasks.remove(task)
    for c in started:
        c.wait_send()


def copy_out(*refs):
    n = (len(refs) - 1) // 2
    copies = [pltpu.make_async_copy(refs[i], refs[n + i], refs[-1].at[i]) for i in range(n)]
    for c in copies:
        c.start()
    for c in copies:
        c.wait()


def slot_tables(in_rows, in_cols, out_rows, out_cols):
    rows, cols = jnp.stack([in_rows, out_rows]), jnp.stack([in_cols, out_cols])
    pair = jnp.where(rows >= 0, (rows % NPAN) * NCOL + cols, NPAN * NCOL)
    slot = jnp.arange(CAP, dtype=jnp.int32)
    hit = pair[:, :, None] == jnp.arange(NPAN * NCOL, dtype=jnp.int32)[None, None, :]
    return pair, jnp.min(jnp.where(hit, slot[None, :, None], CAP), axis=1)


def local(tokens, cotangent, w_in, w_out, in_rows, in_cols, out_rows, out_cols):
    smem = pl.BlockSpec(memory_space=pltpu.SMEM)
    hbm = pl.BlockSpec(memory_space=pl.ANY)
    vmem = pl.BlockSpec(memory_space=pltpu.VMEM)
    rows = tokens.shape[0]
    shapes = [(rows, D), (rows, D), (CAP * 128, 128), (CAP * 128, 128)]
    slot_pair, pair_slot = slot_tables(in_rows, in_cols, out_rows, out_cols)
    half = CAP * 64
    results = pl.pallas_call(
        kernel,
        out_shape=tuple(pltpu.VMEM(s, BF16) for s in shapes),
        in_specs=[hbm, hbm, hbm, hbm, smem, smem],
        out_specs=(vmem,) * 4,
        scratch_shapes=[
            pltpu.VMEM((2, rows, D), BF16),
            pltpu.VMEM((2, NY, NZ, 16, 1024), BF16),
            pltpu.VMEM((2, NY, 16, D), BF16),
            pltpu.VMEM((2, 16, 1024), F32),
            pltpu.VMEM((2, 16, D), F32),
            pltpu.VMEM((16, D // 2), F32),
            pltpu.VMEM((NZ, 16, D // 8), F32),
            pltpu.VMEM((2, CAP + 1, 128, 128), BF16),
            pltpu.VMEM((2, 512, D), BF16),
            pltpu.VMEM((2, NCOL, 128, 128), BF16),
            pltpu.VMEM((2, NPAN + 1, 128, 128), BF16),
            pltpu.VMEM((2, 128, 512), BF16),
            pltpu.VMEM((2, 2, NY, 16, D // 2), BF16),
            pltpu.VMEM((2, 2, 4, 16, D // 2), BF16),
            pltpu.VMEM((2, 2, 4, 16, D // 2), BF16),
            pltpu.VMEM((2, 2, NZ, 16, D // 8), BF16),
            pltpu.VMEM((2, 2, NZ, 16, D // 8), BF16),
            pltpu.VMEM((2, CAP * 128, 128), BF16),
            pltpu.VMEM((4, half // 2, 128), BF16),
            pltpu.VMEM((4, 2, half // 8, 128), BF16),
            pltpu.VMEM((4, 2, half // 16, 128), BF16),
            pltpu.VMEM((4, 2, half // 16, 128), BF16),
            pltpu.VMEM((512, 128), F32),
            pltpu.SemaphoreType.DMA((SEMS,)),
            pltpu.SemaphoreType.DMA((SEMS,)),
            pltpu.SemaphoreType.DMA((4,)),
        ],
        compiler_params=pltpu.CompilerParams(
            collective_id=0, has_side_effects=True, vmem_limit_bytes=52 * 2**20
        ),
    )(tokens, cotangent, w_in, w_out, pair_slot, slot_pair)
    mixed, igrad, ing, outg = pl.pallas_call(
        copy_out,
        out_shape=tuple(jax.ShapeDtypeStruct(s, BF16) for s in shapes),
        in_specs=[vmem] * 4,
        out_specs=(hbm,) * 4,
        scratch_shapes=[pltpu.SemaphoreType.DMA((4,))],
        compiler_params=pltpu.CompilerParams(has_side_effects=True),
    )(*(pltpu.with_memory_space_constraint(r, pltpu.VMEM) for r in results))
    return mixed, igrad, ing.reshape(CAP, 128, 128), outg.reshape(CAP, 128, 128)


def solution(mesh):
    placed = (
        P(("dp", "fsdp"), None),
        P(("dp", "fsdp"), None),
        P("fsdp", None, None),
        P("fsdp", None, None),
        P("fsdp"),
        P("fsdp"),
        P("fsdp"),
        P("fsdp"),
    )
    return jax.shard_map(
        local,
        mesh=mesh,
        in_specs=placed,
        out_specs=(
            P(("dp", "fsdp"), None),
            P(("dp", "fsdp"), None),
            P("fsdp", None, None),
            P("fsdp", None, None),
        ),
        check_vma=False,
    )
```

```python
import jax
import jax.numpy as jnp
from jax import lax
from jax.experimental import pallas as pl
from jax.experimental.pallas import tpu as pltpu
from jax.sharding import PartitionSpec as P

MESH = pl.DeviceIdType.MESH
F32 = jnp.float32
BF16 = jnp.bfloat16

NY, NZ = 8, 4
CAP = 36
NCOL = 32
NPAN = 4
D = 4096
SEMS = 136


def mo(v, m=16):
    return pl.multiple_of(v, m)


def kernel(
    tok, cot, w_in, w_out, pair_slot, slot_pair,
    mixed_o, igrad_o, ing_o, outg_o,
    own, xg, x, t1, t2, t3, t4, ws, wd, xb, hd, acts, prt, rland, lland, zs, zl, g, lc, l1, l2, l3, slope_ref,
    ssem, rsem, lsem,
):
    dp, fs = lax.axis_index("dp"), lax.axis_index("fsdp")
    y, zh = fs // NZ, fs % NZ
    px, zlo, core = dp // 4, (dp // 2) % 2, dp % 2

    def dev(d=dp, f=fs):
        return (d, f)

    up, down, across = (dev(f=y * NZ + (zh + d) % NZ) for d in (1, 3, 2))
    z_routes = ((1, up, 2), (2, down, 1), (3, across, 3))
    right = dev(f=((y + 1) % NY) * NZ + zh)
    left = dev(f=((y + NY - 1) % NY) * NZ + zh)
    core_dev = dev(d=dp + 1 - 2 * core)
    xpa = px + 1 - 2 * (px % 2)
    xpb = (px + 2 * (px % 2) + 3) % 4
    xa_dev = dev(d=xpa * 4 + dp % 4)
    xb_dev = dev(d=xpb * 4 + dp % 4)
    zlo_dev = dev(d=dp + 2 - 4 * zlo)
    everyone = [up, down, across, right, left, core_dev, xa_dev, xb_dev, zlo_dev]

    used = [0]
    started = []

    def send(src, dst, to):
        i = used[0]
        used[0] += 1
        assert i < SEMS
        c = pltpu.make_async_remote_copy(
            src, dst, ssem.at[i], rsem.at[i], device_id=to, device_id_type=MESH
        )
        c.start()
        started.append(c)
        return c

    barrier = pltpu.get_barrier_semaphore()
    for to in everyone:
        pl.semaphore_signal(barrier, inc=1, device_id=to, device_id_type=MESH)

    fetch = [
        pltpu.make_async_copy(src, own.at[a], lsem.at[2 + a])
        for a, src in enumerate((tok, cot))
    ]
    weights = [
        pltpu.make_async_copy(w, ws.at[a, pl.ds(0, CAP)], lsem.at[a])
        for a, w in enumerate((w_in, w_out))
    ]
    for c in fetch + weights:
        c.start()

    for a in range(2):
        fetch[a].wait()
        for k in range(4):
            t1[a, 4 * k : 4 * k + 4, :] = own[a, :, 1024 * k : 1024 * (k + 1)].astype(F32)
        xg[a, y, 0] = t1[a].astype(BF16)

    pl.semaphore_wait(barrier, len(everyone))

    zsend = [
        [send(xg.at[a, y, 0], xg.at[a, y, there], to) for _, to, there in z_routes[:2]]
        for a in range(2)
    ]
    for a in range(2):
        ws[a, CAP] = jnp.zeros((128, 128), BF16)
        hd[a, NPAN] = jnp.zeros((128, 128), BF16)

    def unfold(a, b):
        for d in range(NZ):
            t1[a] = xg[a, b, d].astype(F32)
            for k in range(4):
                t2[a, 4 * d : 4 * d + 4, 1024 * k : 1024 * (k + 1)] = t1[a, 4 * k : 4 * k + 4, :]
        rows = t2[a].astype(BF16)
        x[a, b] = rows
        for c in range(NCOL):
            xb[a, c, pl.ds(mo(b * 16), 16), :] = rows[:, 128 * c : 128 * (c + 1)]

    groups = (pl.ds(0, 1), pl.ds(1, 2), pl.ds(3, 1))
    rights, lefts = (4, 3), (3, 4)
    chains = {}

    def hop(grp, k, arrays=(0, 1)):
        for a in arrays:
            for way, to, n, back in (
                (0, right, rights[(a + grp) % 2], NY - 1),
                (1, left, lefts[(a + grp) % 2], 1),
            ):
                chain = chains.setdefault((a, grp, way), [])
                if k < n:
                    if k:
                        chain[k - 1].wait_recv()
                    ref = xg.at[a, (y + back * k) % NY, groups[grp]]
                    chain.append(send(ref, ref, to))

    def z_near(a):
        for c in zsend[a]:
            c.wait_recv()
        here, to = ((1, down), (2, up))[a]
        zsend[a].append(send(xg.at[a, y, here], xg.at[a, y, 3], to))
        hop(1, 0, (a,))

    def z_far(a):
        zsend[a][2].wait_recv()
        hop(2, 0, (a,))

    def arrive(a, k):
        for grp in range(3):
            for way in range(2):
                chain = chains[(a, grp, way)]
                if k == len(chain):
                    chain[k - 1].wait_recv()
        unfold(a, (y + NY - k) % NY)
        if 2 * k != NY and k:
            unfold(a, (y + k) % NY)

    def dense(a):
        if a == 0:
            for w in weights:
                w.wait()

        def one(c, _):
            for p in range(NPAN):
                slot = pair_slot[a, p * NCOL + c]
                wd[a, pl.ds(p * 128, 128), pl.ds(mo(c * 128, 128), 128)] = ws[a, slot]
            return 0

        lax.fori_loop(0, NCOL, one, 0)

    hop(0, 0)
    dense(0)
    hop(0, 1)
    z_near(0)
    z_near(1)
    hop(0, 2)
    z_far(0)
    z_far(1)
    hop(1, 1)
    dense(1)
    hop(0, 3)
    hop(2, 1)
    hop(1, 2)
    arrive(0, 0)
    arrive(1, 0)
    hop(2, 2)
    arrive(0, 1)
    arrive(1, 1)
    hop(1, 3)
    arrive(0, 2)
    hop(2, 3)
    arrive(1, 2)
    arrive(0, 3)
    arrive(1, 3)
    arrive(0, 4)

    nt = (((1,), (1,)), ((), ()))

    def by_panel(a):
        return lax.dot_general(wd[a], x[a].reshape(128, D), nt, preferred_element_type=F32)

    def grads(dst, half):
        a = 1 - dst

        def one(i, _):
            s = i + half * (CAP // 2)
            pair = slot_pair[a, s]
            blk = jnp.dot(hd[dst, pair // NCOL], xb[a, pair % NCOL], preferred_element_type=F32)
            g[dst, pl.ds(mo(s * 128, 128), 128), :] = blk.astype(BF16)
            return 0

        lax.fori_loop(0, CAP // 2, one, 0, unroll=True)

    half_d = D // 2

    def by_token(side):
        acts[side] = hd[side, :NPAN].reshape(512, 128).astype(F32).T.astype(BF16)

    def partial(a, half):
        for n in range(0, half_d, 512):
            at = half * half_d + n
            part = jnp.dot(acts[a], wd[1 - a, :, at : at + 512], preferred_element_type=F32)
            prt[a, half, :, :, n : n + 512] = part.astype(BF16).reshape(NY, 16, 512)

    def scatter(a, half):
        own_part, from_left, from_right = prt.at[a, half], rland.at[a, half], lland.at[a, half]
        send_z, land_z = zs.at[a, half], zl.at[a, half]
        nr, nl = rights[a ^ half], lefts[a ^ half]
        ways = (
            ([send(own_part.at[(y + nr) % NY], from_left.at[0], right)], from_left, nr, right, 1),
            ([send(own_part.at[(y + NY - nl) % NY], from_right.at[0], left)], from_right, nl, left, NY - 1),
        )
        for k in range(1, 4):
            yield
            for chain, land, n, to, sign in ways:
                if k < n:
                    chain[k - 1].wait_recv()
                    mine = own_part[(y + sign * (n - k)) % NY].astype(F32)
                    land[k - 1] = (mine + land[k - 1].astype(F32)).astype(BF16)
                    chain.append(send(land.at[k - 1], land.at[k], to))
        yield
        for chain, _, _, _, _ in ways:
            chain[-1].wait_recv()
        t3[...] = (
            own_part[y].astype(F32)
            + from_left[nr - 1].astype(F32)
            + from_right[nl - 1].astype(F32)
        )
        w = half_d // 4
        for d in range(NZ):
            for k in range(4):
                t4[d, 4 * k : 4 * k + 4, :] = t3[4 * d : 4 * d + 4, w * k : w * (k + 1)]
            send_z[d] = t4[d].astype(BF16)
        out = [
            send(send_z.at[here], land_z.at[there], to) for here, to, there in z_routes
        ]
        yield
        for c in out:
            c.wait_recv()
        total = send_z[0].astype(F32)
        for d in (1, 2, 3):
            total = total + land_z[d].astype(F32)
        t4[0] = total
        dst = (mixed_o, igrad_o)[a]
        for k in range(4):
            at = half * half_d + w * k
            dst[:, at : at + w] = t4[0, 4 * k : 4 * k + 4, :].astype(BF16)

    ha1, ha2 = ((px + 1) // 2) % 2, px // 2
    hb1, hb2 = px // 2, px % 2
    half_rows = CAP * 64
    n1, n2, n3, n4 = (half_rows // m for m in (2, 4, 8, 16))

    def rows(ref, r, n):
        return ref.at[pl.ds(mo(r), n)]

    def reduce(a, half):
        i = 2 * a + half
        ga, fo = g.at[a], (outg_o, ing_o)[a]
        base = half * half_rows + core * n1
        other = half * half_rows + n1 - core * n1
        ra1 = base + ha1 * n3
        sa1 = base + n3 - ha1 * n3
        ra2 = ra1 + ha2 * n4
        sa2 = ra1 + n4 - ha2 * n4
        rb1 = base + n2 + hb1 * n3
        sb1 = base + n2 + n3 - hb1 * n3
        rb2 = rb1 + hb2 * n4
        sb2 = rb1 + n4 - hb2 * n4

        def add(r, n, land):
            def one(c, _):
                at = pl.ds(mo(r + c * n4), n4)
                got = land[pl.ds(mo(c * n4), n4)].astype(F32)
                g[a, at] = (g[a, at].astype(F32) + got).astype(BF16)
                return 0

            lax.fori_loop(0, n // n4, one, 0)

        c0 = send(rows(ga, other, n1), lc.at[i], core_dev)
        yield
        c0.wait_recv()
        add(base, n1, lc.at[i])
        c1 = send(rows(ga, sa1, n3), l1.at[i, 0], xa_dev)
        c2 = send(rows(ga, sb1, n3), l1.at[i, 1], xb_dev)
        yield
        c1.wait_recv()
        add(ra1, n3, l1.at[i, 0])
        c3 = send(rows(ga, sa2, n4), l2.at[i, 0], xb_dev)
        c2.wait_recv()
        add(rb1, n3, l1.at[i, 1])
        c4 = send(rows(ga, sb2, n4), l2.at[i, 1], xa_dev)
        yield
        c3.wait_recv()
        add(ra2, n4, l2.at[i, 0])
        c4.wait_recv()
        add(rb2, n4, l2.at[i, 1])
        c5 = send(rows(ga, ra2, n4), l3.at[i, 0], zlo_dev)
        c6 = send(rows(ga, rb2, n4), l3.at[i, 1], zlo_dev)
        yield
        for c, r, land in ((c5, ra2, l3.at[i, 0]), (c6, rb2, l3.at[i, 1])):
            c.wait_recv()
            both = g[a, pl.ds(mo(r), n4)].astype(F32) + land[...].astype(F32)
            fo[pl.ds(mo(r), n4)] = both.astype(BF16)
        c7 = send(rows(fo, ra2, n4), rows(fo, ra2, n4), xb_dev)
        c8 = send(rows(fo, rb2, n4), rows(fo, rb2, n4), xa_dev)
        yield
        c7.wait_recv()
        c9 = send(rows(fo, ra1, n3), rows(fo, ra1, n3), xa_dev)
        c8.wait_recv()
        c10 = send(rows(fo, rb1, n3), rows(fo, rb1, n3), xb_dev)
        yield
        c9.wait_recv()
        c10.wait_recv()
        c11 = send(rows(fo, base, n1), rows(fo, base, n1), core_dev)
        yield
        c11.wait_recv()

    def step(task):
        next(task, None)

    red = [reduce(i // 2, i % 2) for i in range(4)]
    sca = [[scatter(a, half) for half in range(2)] for a in range(2)]

    def activate():
        pre = by_panel(0)
        cdf = 0.5 * (1.0 + lax.erf(pre * 0.7071067811865476))
        hd[0, :NPAN] = (pre * cdf).astype(BF16).reshape(NPAN, 128, 128)
        slope_ref[...] = cdf + pre * jnp.exp(-0.5 * pre * pre) * 0.3989422804014327
        by_token(0)

    def differentiate():
        hd[1, :NPAN] = (by_panel(1) * slope_ref[...]).astype(BF16).reshape(NPAN, 128, 128)
        by_token(1)

    activate()
    arrive(1, 4)
    grads(0, 0)
    step(red[0])
    grads(0, 1)
    step(red[1])
    differentiate()
    partial(1, 0)
    partial(1, 1)
    step(red[0])
    step(sca[1][1])
    step(sca[1][0])
    grads(1, 0)
    grads(1, 1)
    step(red[3])
    step(red[1])
    step(red[2])
    partial(0, 1)
    step(sca[0][1])
    partial(0, 0)
    step(red[3])
    step(sca[0][0])
    step(red[0])
    step(sca[1][1])
    step(red[2])
    step(sca[1][0])
    step(red[1])
    step(sca[0][1])
    step(red[3])
    step(sca[0][0])
    step(red[0])
    step(sca[1][1])
    step(red[2])
    step(red[1])
    step(sca[1][0])
    step(red[3])
    step(sca[0][1])
    step(red[0])
    step(red[2])
    step(sca[0][0])
    step(red[1])
    step(sca[1][1])
    step(red[0])
    step(red[3])
    step(sca[1][0])
    step(sca[0][1])
    step(red[2])
    step(red[1])
    step(sca[0][0])
    step(red[0])
    step(sca[1][1])
    step(red[3])
    step(sca[1][0])
    step(red[2])
    step(sca[0][1])
    step(sca[0][0])
    step(red[1])
    step(red[0])
    step(red[3])
    step(sca[1][1])
    step(red[1])
    step(sca[1][0])
    step(red[2])
    step(red[3])
    step(sca[0][1])
    step(sca[0][0])
    step(red[2])
    for c in started:
        c.wait_send()


def copy_out(*refs):
    n = (len(refs) - 1) // 2
    copies = [pltpu.make_async_copy(refs[i], refs[n + i], refs[-1].at[i]) for i in range(n)]
    for c in copies:
        c.start()
    for c in copies:
        c.wait()


def slot_tables(in_rows, in_cols, out_rows, out_cols):
    rows, cols = jnp.stack([in_rows, out_rows]), jnp.stack([in_cols, out_cols])
    pair = jnp.where(rows >= 0, (rows % NPAN) * NCOL + cols, NPAN * NCOL)
    slot = jnp.arange(CAP, dtype=jnp.int32)
    hit = pair[:, :, None] == jnp.arange(NPAN * NCOL, dtype=jnp.int32)[None, None, :]
    return pair, jnp.min(jnp.where(hit, slot[None, :, None], CAP), axis=1)


def near(value):
    return pltpu.with_memory_space_constraint(value, pltpu.VMEM)


def local(tokens, cotangent, w_in, w_out, in_rows, in_cols, out_rows, out_cols):
    smem = pl.BlockSpec(memory_space=pltpu.SMEM)
    hbm = pl.BlockSpec(memory_space=pl.ANY)
    vmem = pl.BlockSpec(memory_space=pltpu.VMEM)
    rows = tokens.shape[0]
    shapes = [(rows, D), (rows, D), (CAP * 128, 128), (CAP * 128, 128)]
    slot_pair, pair_slot = slot_tables(in_rows, in_cols, out_rows, out_cols)
    half = CAP * 64
    results = pl.pallas_call(
        kernel,
        out_shape=tuple(pltpu.VMEM(s, BF16) for s in shapes),
        in_specs=[hbm, hbm, hbm, hbm, smem, smem],
        out_specs=(vmem,) * 4,
        scratch_shapes=[
            pltpu.VMEM((2, rows, D), BF16),
            pltpu.VMEM((2, NY, NZ, 16, 1024), BF16),
            pltpu.VMEM((2, NY, 16, D), BF16),
            pltpu.VMEM((2, 16, 1024), F32),
            pltpu.VMEM((2, 16, D), F32),
            pltpu.VMEM((16, D // 2), F32),
            pltpu.VMEM((NZ, 16, D // 8), F32),
            pltpu.VMEM((2, CAP + 1, 128, 128), BF16),
            pltpu.VMEM((2, 512, D), BF16),
            pltpu.VMEM((2, NCOL, 128, 128), BF16),
            pltpu.VMEM((2, NPAN + 1, 128, 128), BF16),
            pltpu.VMEM((2, 128, 512), BF16),
            pltpu.VMEM((2, 2, NY, 16, D // 2), BF16),
            pltpu.VMEM((2, 2, 4, 16, D // 2), BF16),
            pltpu.VMEM((2, 2, 4, 16, D // 2), BF16),
            pltpu.VMEM((2, 2, NZ, 16, D // 8), BF16),
            pltpu.VMEM((2, 2, NZ, 16, D // 8), BF16),
            pltpu.VMEM((2, CAP * 128, 128), BF16),
            pltpu.VMEM((4, half // 2, 128), BF16),
            pltpu.VMEM((4, 2, half // 8, 128), BF16),
            pltpu.VMEM((4, 2, half // 16, 128), BF16),
            pltpu.VMEM((4, 2, half // 16, 128), BF16),
            pltpu.VMEM((512, 128), F32),
            pltpu.SemaphoreType.DMA((SEMS,)),
            pltpu.SemaphoreType.DMA((SEMS,)),
            pltpu.SemaphoreType.DMA((4,)),
        ],
        compiler_params=pltpu.CompilerParams(
            collective_id=0, has_side_effects=True, vmem_limit_bytes=52 * 2**20
        ),
    )(tokens, cotangent, w_in, w_out, pair_slot, slot_pair)
    mixed, igrad, ing, outg = pl.pallas_call(
        copy_out,
        out_shape=tuple(jax.ShapeDtypeStruct(s, BF16) for s in shapes),
        in_specs=[vmem] * 4,
        out_specs=(hbm,) * 4,
        scratch_shapes=[pltpu.SemaphoreType.DMA((4,))],
        compiler_params=pltpu.CompilerParams(has_side_effects=True),
    )(*map(near, results))
    return mixed, igrad, ing.reshape(CAP, 128, 128), outg.reshape(CAP, 128, 128)


def solution(mesh):
    placed = (
        P(("dp", "fsdp"), None),
        P(("dp", "fsdp"), None),
        P("fsdp", None, None),
        P("fsdp", None, None),
        P("fsdp"),
        P("fsdp"),
        P("fsdp"),
        P("fsdp"),
    )
    return jax.shard_map(
        local,
        mesh=mesh,
        in_specs=placed,
        out_specs=(
            P(("dp", "fsdp"), None),
            P(("dp", "fsdp"), None),
            P("fsdp", None, None),
            P("fsdp", None, None),
        ),
        check_vma=False,
    )
```

```python
import jax
import jax.numpy as jnp
from jax import lax
from jax.experimental import pallas as pl
from jax.experimental.pallas import tpu as pltpu
from jax.sharding import PartitionSpec as P

MESH = pl.DeviceIdType.MESH
F32 = jnp.float32
BF16 = jnp.bfloat16

NY, NZ = 8, 4
CAP = 36
NCOL = 32
NPAN = 4
D = 4096
SEMS = 136


def mo(v, m=16):
    return pl.multiple_of(v, m)


def kernel(
    tok, cot, w_in, w_out, in_rows, in_cols, out_rows, out_cols,
    mixed_o, igrad_o, ing_o, outg_o,
    own, xg, x, t1, t2, t3, t4, ws, wd, xb, hd, acts, prt, rland, lland, zs, zl, g, lc, l1, l2, l3, slope_ref, table, pair_slot,
    ssem, rsem, lsem,
):
    dp, fs = lax.axis_index("dp"), lax.axis_index("fsdp")
    y, zh = fs // NZ, fs % NZ
    px, zlo, core = dp // 4, (dp // 2) % 2, dp % 2

    def dev(d=dp, f=fs):
        return (d, f)

    up, down, across = (dev(f=y * NZ + (zh + d) % NZ) for d in (1, 3, 2))
    z_routes = ((1, up, 2), (2, down, 1), (3, across, 3))
    right = dev(f=((y + 1) % NY) * NZ + zh)
    left = dev(f=((y + NY - 1) % NY) * NZ + zh)
    core_dev = dev(d=dp + 1 - 2 * core)
    xpa = px + 1 - 2 * (px % 2)
    xpb = (px + 2 * (px % 2) + 3) % 4
    xa_dev = dev(d=xpa * 4 + dp % 4)
    xb_dev = dev(d=xpb * 4 + dp % 4)
    zlo_dev = dev(d=dp + 2 - 4 * zlo)
    everyone = [up, down, across, right, left, core_dev, xa_dev, xb_dev, zlo_dev]

    used = [0]
    started = []

    def send(src, dst, to):
        i = used[0]
        used[0] += 1
        assert i < SEMS
        c = pltpu.make_async_remote_copy(
            src, dst, ssem.at[i], rsem.at[i], device_id=to, device_id_type=MESH
        )
        c.start()
        started.append(c)
        return c

    fetch = [
        pltpu.make_async_copy(src, own.at[a], lsem.at[2 + a])
        for a, src in enumerate((tok, cot))
    ]
    weights = [
        pltpu.make_async_copy(w, ws.at[a, pl.ds(0, CAP)], lsem.at[a])
        for a, w in enumerate((w_in, w_out))
    ]
    for c in fetch:
        c.start()

    barrier = pltpu.get_barrier_semaphore()
    for to in everyone:
        pl.semaphore_signal(barrier, inc=1, device_id=to, device_id_type=MESH)
    for c in weights:
        c.start()

    for a in range(2):
        fetch[a].wait()
        for k in range(4):
            t1[a, 4 * k : 4 * k + 4, :] = own[a, :, 1024 * k : 1024 * (k + 1)].astype(F32)
        xg[a, y, 0] = t1[a].astype(BF16)

    pl.semaphore_wait(barrier, len(everyone))

    zsend = [
        [send(xg.at[a, y, 0], xg.at[a, y, there], to) for _, to, there in z_routes[:2]]
        for a in range(2)
    ]
    for a in range(2):
        ws[a, CAP] = jnp.zeros((128, 128), BF16)
        hd[a, NPAN] = jnp.zeros((128, 128), BF16)

    def unfold(a, b):
        for d in range(NZ):
            t1[a] = xg[a, b, d].astype(F32)
            for k in range(4):
                t2[a, 4 * d : 4 * d + 4, 1024 * k : 1024 * (k + 1)] = t1[a, 4 * k : 4 * k + 4, :]
        rows = t2[a].astype(BF16)
        x[a, b] = rows
        for c in range(NCOL):
            xb[a, c, pl.ds(mo(b * 16), 16), :] = rows[:, 128 * c : 128 * (c + 1)]

    groups = (pl.ds(0, 1), pl.ds(1, 2), pl.ds(3, 1))
    rights, lefts = (4, 3), (3, 4)
    chains = {}

    def hop(grp, k, arrays=(0, 1)):
        for a in arrays:
            for way, to, n, back in (
                (0, right, rights[(a + grp) % 2], NY - 1),
                (1, left, lefts[(a + grp) % 2], 1),
            ):
                chain = chains.setdefault((a, grp, way), [])
                if k < n:
                    if k:
                        chain[k - 1].wait_recv()
                    ref = xg.at[a, (y + back * k) % NY, groups[grp]]
                    chain.append(send(ref, ref, to))

    def z_near(a):
        for c in zsend[a]:
            c.wait_recv()
        here, to = ((1, down), (2, up))[a]
        zsend[a].append(send(xg.at[a, y, here], xg.at[a, y, 3], to))
        hop(1, 0, (a,))

    def z_far(a):
        zsend[a][2].wait_recv()
        hop(2, 0, (a,))

    def arrive(a, k):
        for grp in range(3):
            for way in range(2):
                chain = chains[(a, grp, way)]
                if k == len(chain):
                    chain[k - 1].wait_recv()
        unfold(a, (y + NY - k) % NY)
        if 2 * k != NY and k:
            unfold(a, (y + k) % NY)

    def dense(a):
        if a == 0:
            for w in weights:
                w.wait()

        def one(c, _):
            for p in range(NPAN):
                slot = pair_slot[a, 0, p * NCOL + c]
                wd[a, pl.ds(p * 128, 128), pl.ds(mo(c * 128, 128), 128)] = ws[a, slot]
            return 0

        lax.fori_loop(0, NCOL, one, 0)

    hop(0, 0)

    lane = lax.broadcasted_iota(jnp.int32, (8, 128), 1)
    for a, (rows, cols) in enumerate(((in_rows, in_cols), (out_rows, out_cols))):

        def find(s, found, rows=rows, cols=cols):
            live = (rows[s] + 128) // 128
            code = live * (rows[s] % NPAN * NCOL + cols[s]) + (1 - live) * (NPAN * NCOL)
            return jnp.where(lane == code, s, found)

        table[a] = lax.fori_loop(0, CAP, find, jnp.full((8, 128), CAP, jnp.int32))
    to_scalars = pltpu.make_async_copy(table, pair_slot, lsem.at[4])
    to_scalars.start()
    to_scalars.wait()
    dense(0)
    hop(0, 1)
    z_near(0)
    z_near(1)
    hop(0, 2)
    z_far(0)
    z_far(1)
    hop(1, 1)
    dense(1)
    hop(0, 3)
    hop(2, 1)
    hop(1, 2)
    arrive(0, 0)
    arrive(1, 0)
    hop(2, 2)
    arrive(0, 1)
    arrive(1, 1)
    hop(1, 3)
    arrive(0, 2)
    hop(2, 3)
    arrive(1, 2)
    arrive(0, 3)
    arrive(1, 3)
    arrive(0, 4)

    nt = (((1,), (1,)), ((), ()))

    def by_panel(a):
        return lax.dot_general(wd[a], x[a].reshape(128, D), nt, preferred_element_type=F32)

    def grads(dst, half):
        a = 1 - dst
        rows, cols = ((out_rows, out_cols), (in_rows, in_cols))[dst]

        def one(i, _):
            s = i + half * (CAP // 2)
            live = (rows[s] + 128) // 128
            panel = NPAN - live * (NPAN - rows[s] % NPAN)
            blk = jnp.dot(hd[dst, panel], xb[a, live * cols[s]], preferred_element_type=F32)
            g[dst, pl.ds(mo(s * 128, 128), 128), :] = blk.astype(BF16)
            return 0

        lax.fori_loop(0, CAP // 2, one, 0, unroll=True)

    half_d = D // 2

    def by_token(side):
        acts[side] = hd[side, :NPAN].reshape(512, 128).astype(F32).T.astype(BF16)

    def partial(a, half):
        for n in range(0, half_d, 512):
            at = half * half_d + n
            part = jnp.dot(acts[a], wd[1 - a, :, at : at + 512], preferred_element_type=F32)
            prt[a, half, :, :, n : n + 512] = part.astype(BF16).reshape(NY, 16, 512)

    def scatter(a, half):
        own_part, from_left, from_right = prt.at[a, half], rland.at[a, half], lland.at[a, half]
        send_z, land_z = zs.at[a, half], zl.at[a, half]
        nr, nl = rights[a ^ half], lefts[a ^ half]
        ways = (
            ([send(own_part.at[(y + nr) % NY], from_left.at[0], right)], from_left, nr, right, 1),
            ([send(own_part.at[(y + NY - nl) % NY], from_right.at[0], left)], from_right, nl, left, NY - 1),
        )
        for k in range(1, 4):
            yield
            for chain, land, n, to, sign in ways:
                if k < n:
                    chain[k - 1].wait_recv()
                    mine = own_part[(y + sign * (n - k)) % NY].astype(F32)
                    land[k - 1] = (mine + land[k - 1].astype(F32)).astype(BF16)
                    chain.append(send(land.at[k - 1], land.at[k], to))
        yield
        for chain, _, _, _, _ in ways:
            chain[-1].wait_recv()
        t3[...] = (
            own_part[y].astype(F32)
            + from_left[nr - 1].astype(F32)
            + from_right[nl - 1].astype(F32)
        )
        w = half_d // 4
        for d in range(NZ):
            for k in range(4):
                t4[d, 4 * k : 4 * k + 4, :] = t3[4 * d : 4 * d + 4, w * k : w * (k + 1)]
            send_z[d] = t4[d].astype(BF16)
        out = [
            send(send_z.at[here], land_z.at[there], to) for here, to, there in z_routes
        ]
        yield
        for c in out:
            c.wait_recv()
        total = send_z[0].astype(F32)
        for d in (1, 2, 3):
            total = total + land_z[d].astype(F32)
        t4[0] = total
        dst = (mixed_o, igrad_o)[a]
        for k in range(4):
            at = half * half_d + w * k
            dst[:, at : at + w] = t4[0, 4 * k : 4 * k + 4, :].astype(BF16)

    ha1, ha2 = ((px + 1) // 2) % 2, px // 2
    hb1, hb2 = px // 2, px % 2
    half_rows = CAP * 64
    n1, n2, n3, n4 = (half_rows // m for m in (2, 4, 8, 16))

    def rows(ref, r, n):
        return ref.at[pl.ds(mo(r), n)]

    def reduce(a, half):
        i = 2 * a + half
        ga, fo = g.at[a], (outg_o, ing_o)[a]
        base = half * half_rows + core * n1
        other = half * half_rows + n1 - core * n1
        ra1 = base + ha1 * n3
        sa1 = base + n3 - ha1 * n3
        ra2 = ra1 + ha2 * n4
        sa2 = ra1 + n4 - ha2 * n4
        rb1 = base + n2 + hb1 * n3
        sb1 = base + n2 + n3 - hb1 * n3
        rb2 = rb1 + hb2 * n4
        sb2 = rb1 + n4 - hb2 * n4

        def add(r, n, land):
            def one(c, _):
                at = pl.ds(mo(r + c * n4), n4)
                got = land[pl.ds(mo(c * n4), n4)].astype(F32)
                g[a, at] = (g[a, at].astype(F32) + got).astype(BF16)
                return 0

            lax.fori_loop(0, n // n4, one, 0)

        c0 = send(rows(ga, other, n1), lc.at[i], core_dev)
        yield
        c0.wait_recv()
        add(base, n1, lc.at[i])
        c1 = send(rows(ga, sa1, n3), l1.at[i, 0], xa_dev)
        c2 = send(rows(ga, sb1, n3), l1.at[i, 1], xb_dev)
        yield
        c1.wait_recv()
        add(ra1, n3, l1.at[i, 0])
        c3 = send(rows(ga, sa2, n4), l2.at[i, 0], xb_dev)
        c2.wait_recv()
        add(rb1, n3, l1.at[i, 1])
        c4 = send(rows(ga, sb2, n4), l2.at[i, 1], xa_dev)
        yield
        c3.wait_recv()
        add(ra2, n4, l2.at[i, 0])
        c4.wait_recv()
        add(rb2, n4, l2.at[i, 1])
        c5 = send(rows(ga, ra2, n4), l3.at[i, 0], zlo_dev)
        c6 = send(rows(ga, rb2, n4), l3.at[i, 1], zlo_dev)
        yield
        for c, r, land in ((c5, ra2, l3.at[i, 0]), (c6, rb2, l3.at[i, 1])):
            c.wait_recv()
            both = g[a, pl.ds(mo(r), n4)].astype(F32) + land[...].astype(F32)
            fo[pl.ds(mo(r), n4)] = both.astype(BF16)
        c7 = send(rows(fo, ra2, n4), rows(fo, ra2, n4), xb_dev)
        c8 = send(rows(fo, rb2, n4), rows(fo, rb2, n4), xa_dev)
        yield
        c7.wait_recv()
        c9 = send(rows(fo, ra1, n3), rows(fo, ra1, n3), xa_dev)
        c8.wait_recv()
        c10 = send(rows(fo, rb1, n3), rows(fo, rb1, n3), xb_dev)
        yield
        c9.wait_recv()
        c10.wait_recv()
        c11 = send(rows(fo, base, n1), rows(fo, base, n1), core_dev)
        yield
        c11.wait_recv()

    def step(task):
        next(task, None)

    red = [reduce(i // 2, i % 2) for i in range(4)]
    sca = [[scatter(a, half) for half in range(2)] for a in range(2)]

    def activate():
        pre = by_panel(0)
        cdf = 0.5 * (1.0 + lax.erf(pre * 0.7071067811865476))
        hd[0, :NPAN] = (pre * cdf).astype(BF16).reshape(NPAN, 128, 128)
        slope_ref[...] = cdf + pre * jnp.exp(-0.5 * pre * pre) * 0.3989422804014327
        by_token(0)

    def differentiate():
        hd[1, :NPAN] = (by_panel(1) * slope_ref[...]).astype(BF16).reshape(NPAN, 128, 128)
        by_token(1)

    activate()
    arrive(1, 4)
    grads(0, 0)
    step(red[0])
    grads(0, 1)
    step(red[1])
    differentiate()
    partial(1, 0)
    partial(1, 1)
    step(red[0])
    step(sca[1][1])
    step(sca[1][0])
    grads(1, 0)
    grads(1, 1)
    step(red[3])
    step(red[1])
    step(red[2])
    partial(0, 1)
    step(sca[0][1])
    partial(0, 0)
    step(red[3])
    step(sca[0][0])
    step(red[0])
    step(sca[1][1])
    step(red[2])
    step(sca[1][0])
    step(red[1])
    step(sca[0][1])
    step(red[3])
    step(sca[0][0])
    step(red[0])
    step(sca[1][1])
    step(red[2])
    step(red[1])
    step(sca[1][0])
    step(red[3])
    step(sca[0][1])
    step(red[0])
    step(red[2])
    step(sca[0][0])
    step(red[1])
    step(sca[1][1])
    step(red[0])
    step(red[3])
    step(sca[1][0])
    step(sca[0][1])
    step(red[2])
    step(red[1])
    step(sca[0][0])
    step(red[0])
    step(sca[1][1])
    step(red[3])
    step(sca[1][0])
    step(red[2])
    step(sca[0][1])
    step(sca[0][0])
    step(red[1])
    step(red[0])
    step(red[3])
    step(sca[1][1])
    step(red[1])
    step(sca[1][0])
    step(red[2])
    step(red[3])
    step(sca[0][1])
    step(sca[0][0])
    step(red[2])
    for c in started:
        c.wait_send()


def copy_out(*refs):
    n = (len(refs) - 1) // 2
    copies = [pltpu.make_async_copy(refs[i], refs[n + i], refs[-1].at[i]) for i in range(n)]
    for c in copies:
        c.start()
    for c in copies:
        c.wait()


def near(value):
    return pltpu.with_memory_space_constraint(value, pltpu.VMEM)


def local(tokens, cotangent, w_in, w_out, in_rows, in_cols, out_rows, out_cols):
    smem = pl.BlockSpec(memory_space=pltpu.SMEM)
    hbm = pl.BlockSpec(memory_space=pl.ANY)
    vmem = pl.BlockSpec(memory_space=pltpu.VMEM)
    rows = tokens.shape[0]
    shapes = [(rows, D), (rows, D), (CAP * 128, 128), (CAP * 128, 128)]
    half = CAP * 64
    results = pl.pallas_call(
        kernel,
        out_shape=tuple(pltpu.VMEM(s, BF16) for s in shapes),
        in_specs=[hbm] * 4 + [smem] * 4,
        out_specs=(vmem,) * 4,
        scratch_shapes=[
            pltpu.VMEM((2, rows, D), BF16),
            pltpu.VMEM((2, NY, NZ, 16, 1024), BF16),
            pltpu.VMEM((2, NY, 16, D), BF16),
            pltpu.VMEM((2, 16, 1024), F32),
            pltpu.VMEM((2, 16, D), F32),
            pltpu.VMEM((16, D // 2), F32),
            pltpu.VMEM((NZ, 16, D // 8), F32),
            pltpu.VMEM((2, CAP + 1, 128, 128), BF16),
            pltpu.VMEM((2, 512, D), BF16),
            pltpu.VMEM((2, NCOL, 128, 128), BF16),
            pltpu.VMEM((2, NPAN + 1, 128, 128), BF16),
            pltpu.VMEM((2, 128, 512), BF16),
            pltpu.VMEM((2, 2, NY, 16, D // 2), BF16),
            pltpu.VMEM((2, 2, 4, 16, D // 2), BF16),
            pltpu.VMEM((2, 2, 4, 16, D // 2), BF16),
            pltpu.VMEM((2, 2, NZ, 16, D // 8), BF16),
            pltpu.VMEM((2, 2, NZ, 16, D // 8), BF16),
            pltpu.VMEM((2, CAP * 128, 128), BF16),
            pltpu.VMEM((4, half // 2, 128), BF16),
            pltpu.VMEM((4, 2, half // 8, 128), BF16),
            pltpu.VMEM((4, 2, half // 16, 128), BF16),
            pltpu.VMEM((4, 2, half // 16, 128), BF16),
            pltpu.VMEM((512, 128), F32),
            pltpu.VMEM((2, 8, 128), jnp.int32),
            pltpu.SMEM((2, 8, 128), jnp.int32),
            pltpu.SemaphoreType.DMA((SEMS,)),
            pltpu.SemaphoreType.DMA((SEMS,)),
            pltpu.SemaphoreType.DMA((5,)),
        ],
        compiler_params=pltpu.CompilerParams(
            collective_id=0, has_side_effects=True, vmem_limit_bytes=52 * 2**20
        ),
    )(tokens, cotangent, w_in, w_out, in_rows, in_cols, out_rows, out_cols)
    mixed, igrad, ing, outg = pl.pallas_call(
        copy_out,
        out_shape=tuple(jax.ShapeDtypeStruct(s, BF16) for s in shapes),
        in_specs=[vmem] * 4,
        out_specs=(hbm,) * 4,
        scratch_shapes=[pltpu.SemaphoreType.DMA((4,))],
        compiler_params=pltpu.CompilerParams(has_side_effects=True),
    )(*map(near, results))
    return mixed, igrad, ing.reshape(CAP, 128, 128), outg.reshape(CAP, 128, 128)


def solution(mesh):
    placed = (
        P(("dp", "fsdp"), None),
        P(("dp", "fsdp"), None),
        P("fsdp", None, None),
        P("fsdp", None, None),
        P("fsdp"),
        P("fsdp"),
        P("fsdp"),
        P("fsdp"),
    )
    return jax.shard_map(
        local,
        mesh=mesh,
        in_specs=placed,
        out_specs=(
            P(("dp", "fsdp"), None),
            P(("dp", "fsdp"), None),
            P("fsdp", None, None),
            P("fsdp", None, None),
        ),
        check_vma=False,
    )
```

```python
import jax
import jax.numpy as jnp
from jax import lax
from jax.experimental import pallas as pl
from jax.experimental.pallas import tpu as pltpu
from jax.sharding import PartitionSpec as P

MESH = pl.DeviceIdType.MESH
F32 = jnp.float32
BF16 = jnp.bfloat16

NY, NZ = 8, 4
CAP = 36
NCOL = 32
NPAN = 4
D = 4096
SEMS = 136


def mo(v, m=16):
    return pl.multiple_of(v, m)


def kernel(
    tok, cot, w_in, w_out, in_rows, in_cols, out_rows, out_cols,
    mixed_o, igrad_o, ing_o, outg_o,
    own, xg, x, t1, t2, t3, t4, ws, wd, xb, hd, acts, prt, rland, lland, zs, zl, g, lc, l1, l2, l3, slope_ref, table, pair_slot,
    ssem, rsem, lsem,
):
    dp, fs = lax.axis_index("dp"), lax.axis_index("fsdp")
    y, zh = fs // NZ, fs % NZ
    px, zlo, core = dp // 4, (dp // 2) % 2, dp % 2

    def dev(d=dp, f=fs):
        return (d, f)

    up, down, across = (dev(f=y * NZ + (zh + d) % NZ) for d in (1, 3, 2))
    z_routes = ((1, up, 2), (2, down, 1), (3, across, 3))
    right = dev(f=((y + 1) % NY) * NZ + zh)
    left = dev(f=((y + NY - 1) % NY) * NZ + zh)
    core_dev = dev(d=dp + 1 - 2 * core)
    xpa = px + 1 - 2 * (px % 2)
    xpb = (px + 2 * (px % 2) + 3) % 4
    xa_dev = dev(d=xpa * 4 + dp % 4)
    xb_dev = dev(d=xpb * 4 + dp % 4)
    zlo_dev = dev(d=dp + 2 - 4 * zlo)
    everyone = [up, down, across, right, left, core_dev, xa_dev, xb_dev, zlo_dev]

    used = [0]
    started = []

    def send(src, dst, to):
        i = used[0]
        used[0] += 1
        assert i < SEMS
        c = pltpu.make_async_remote_copy(
            src, dst, ssem.at[i], rsem.at[i], device_id=to, device_id_type=MESH
        )
        c.start()
        started.append(c)
        return c

    fetch = [
        pltpu.make_async_copy(src, own.at[a], lsem.at[2 + a])
        for a, src in enumerate((tok, cot))
    ]
    weights = [
        pltpu.make_async_copy(w, ws.at[a, pl.ds(0, CAP)], lsem.at[a])
        for a, w in enumerate((w_in, w_out))
    ]
    for c in fetch:
        c.start()

    barrier = pltpu.get_barrier_semaphore()
    for to in everyone:
        pl.semaphore_signal(barrier, inc=1, device_id=to, device_id_type=MESH)
    for c in weights:
        c.start()

    def fold_own(a):
        fetch[a].wait()
        for k in range(4):
            t1[a, 4 * k : 4 * k + 4, :] = own[a, :, 1024 * k : 1024 * (k + 1)].astype(F32)
        xg[a, y, 0] = t1[a].astype(BF16)

    fold_own(0)
    pl.semaphore_wait(barrier, len(everyone))
    zsend = []
    for a in range(2):
        if a:
            fold_own(a)
        zsend.append([send(xg.at[a, y, 0], xg.at[a, y, there], to) for _, to, there in z_routes[:2]])
    for a in range(2):
        ws[a, CAP] = jnp.zeros((128, 128), BF16)
        hd[a, NPAN] = jnp.zeros((128, 128), BF16)

    def unfold(a, b):
        for d in range(NZ):
            t1[a] = xg[a, b, d].astype(F32)
            for k in range(4):
                t2[a, 4 * d : 4 * d + 4, 1024 * k : 1024 * (k + 1)] = t1[a, 4 * k : 4 * k + 4, :]
        rows = t2[a].astype(BF16)
        x[a, b] = rows
        for c in range(NCOL):
            xb[a, c, pl.ds(mo(b * 16), 16), :] = rows[:, 128 * c : 128 * (c + 1)]

    groups = (pl.ds(0, 1), pl.ds(1, 2), pl.ds(3, 1))
    rights, lefts = (4, 3), (3, 4)
    chains = {}

    def hop(grp, k, arrays=(0, 1)):
        for a in arrays:
            for way, to, n, back in (
                (0, right, rights[(a + grp) % 2], NY - 1),
                (1, left, lefts[(a + grp) % 2], 1),
            ):
                chain = chains.setdefault((a, grp, way), [])
                if k < n:
                    if k:
                        chain[k - 1].wait_recv()
                    ref = xg.at[a, (y + back * k) % NY, groups[grp]]
                    chain.append(send(ref, ref, to))

    def z_near(a):
        for c in zsend[a]:
            c.wait_recv()
        here, to = ((1, down), (2, up))[a]
        zsend[a].append(send(xg.at[a, y, here], xg.at[a, y, 3], to))
        hop(1, 0, (a,))

    def z_far(a):
        zsend[a][2].wait_recv()
        hop(2, 0, (a,))

    def arrive(a, k):
        for grp in range(3):
            for way in range(2):
                chain = chains[(a, grp, way)]
                if k == len(chain):
                    chain[k - 1].wait_recv()
        unfold(a, (y + NY - k) % NY)
        if 2 * k != NY and k:
            unfold(a, (y + k) % NY)

    def dense(a):
        if a == 0:
            for w in weights:
                w.wait()

        def one(c, _):
            for p in range(NPAN):
                slot = pair_slot[a, 0, p * NCOL + c]
                wd[a, pl.ds(p * 128, 128), pl.ds(mo(c * 128, 128), 128)] = ws[a, slot]
            return 0

        lax.fori_loop(0, NCOL, one, 0)

    hop(0, 0)

    lane = lax.broadcasted_iota(jnp.int32, (8, 128), 1)
    for a, (rows, cols) in enumerate(((in_rows, in_cols), (out_rows, out_cols))):

        def find(s, found, rows=rows, cols=cols):
            live = (rows[s] + 128) // 128
            code = live * (rows[s] % NPAN * NCOL + cols[s]) + (1 - live) * (NPAN * NCOL)
            return jnp.where(lane == code, s, found)

        table[a] = lax.fori_loop(0, CAP, find, jnp.full((8, 128), CAP, jnp.int32))
    to_scalars = pltpu.make_async_copy(table, pair_slot, lsem.at[4])
    to_scalars.start()
    to_scalars.wait()
    dense(0)
    hop(0, 1)
    z_near(0)
    z_near(1)
    hop(0, 2)
    z_far(0)
    z_far(1)
    hop(1, 1)
    dense(1)
    hop(0, 3)
    hop(2, 1)
    hop(1, 2)
    arrive(0, 0)
    arrive(1, 0)
    hop(2, 2)
    arrive(0, 1)
    arrive(1, 1)
    hop(1, 3)
    arrive(0, 2)
    hop(2, 3)
    arrive(1, 2)
    arrive(0, 3)
    arrive(1, 3)
    arrive(0, 4)

    nt = (((1,), (1,)), ((), ()))

    def by_panel(a):
        return lax.dot_general(wd[a], x[a].reshape(128, D), nt, preferred_element_type=F32)

    def grads(dst, half):
        a = 1 - dst
        rows, cols = ((out_rows, out_cols), (in_rows, in_cols))[dst]

        def one(i, _):
            s = i + half * (CAP // 2)
            live = (rows[s] + 128) // 128
            panel = NPAN - live * (NPAN - rows[s] % NPAN)
            blk = jnp.dot(hd[dst, panel], xb[a, live * cols[s]], preferred_element_type=F32)
            g[dst, pl.ds(mo(s * 128, 128), 128), :] = blk.astype(BF16)
            return 0

        lax.fori_loop(0, CAP // 2, one, 0, unroll=True)

    half_d = D // 2

    def by_token(side):
        acts[side] = hd[side, :NPAN].reshape(512, 128).astype(F32).T.astype(BF16)

    def partial(a, half):
        for n in range(0, half_d, 512):
            at = half * half_d + n
            part = jnp.dot(acts[a], wd[1 - a, :, at : at + 512], preferred_element_type=F32)
            prt[a, half, :, :, n : n + 512] = part.astype(BF16).reshape(NY, 16, 512)

    def scatter(a, half):
        own_part, from_left, from_right = prt.at[a, half], rland.at[a, half], lland.at[a, half]
        send_z, land_z = zs.at[a, half], zl.at[a, half]
        nr, nl = rights[a ^ half], lefts[a ^ half]
        ways = (
            ([send(own_part.at[(y + nr) % NY], from_left.at[0], right)], from_left, nr, right, 1),
            ([send(own_part.at[(y + NY - nl) % NY], from_right.at[0], left)], from_right, nl, left, NY - 1),
        )
        for k in range(1, 4):
            yield
            for chain, land, n, to, sign in ways:
                if k < n:
                    chain[k - 1].wait_recv()
                    mine = own_part[(y + sign * (n - k)) % NY].astype(F32)
                    land[k - 1] = (mine + land[k - 1].astype(F32)).astype(BF16)
                    chain.append(send(land.at[k - 1], land.at[k], to))
        yield
        for chain, _, _, _, _ in ways:
            chain[-1].wait_recv()
        t3[...] = (
            own_part[y].astype(F32)
            + from_left[nr - 1].astype(F32)
            + from_right[nl - 1].astype(F32)
        )
        w = half_d // 4
        for d in range(NZ):
            for k in range(4):
                t4[d, 4 * k : 4 * k + 4, :] = t3[4 * d : 4 * d + 4, w * k : w * (k + 1)]
            send_z[d] = t4[d].astype(BF16)
        out = [
            send(send_z.at[here], land_z.at[there], to) for here, to, there in z_routes
        ]
        yield
        for c in out:
            c.wait_recv()
        total = send_z[0].astype(F32)
        for d in (1, 2, 3):
            total = total + land_z[d].astype(F32)
        t4[0] = total
        dst = (mixed_o, igrad_o)[a]
        for k in range(4):
            at = half * half_d + w * k
            dst[:, at : at + w] = t4[0, 4 * k : 4 * k + 4, :].astype(BF16)

    ha1, ha2 = ((px + 1) // 2) % 2, px // 2
    hb1, hb2 = px // 2, px % 2
    half_rows = CAP * 64
    n1, n2, n3, n4 = (half_rows // m for m in (2, 4, 8, 16))

    def rows(ref, r, n):
        return ref.at[pl.ds(mo(r), n)]

    def reduce(a, half):
        i = 2 * a + half
        ga, fo = g.at[a], (outg_o, ing_o)[a]
        base = half * half_rows + core * n1
        other = half * half_rows + n1 - core * n1
        ra1 = base + ha1 * n3
        sa1 = base + n3 - ha1 * n3
        ra2 = ra1 + ha2 * n4
        sa2 = ra1 + n4 - ha2 * n4
        rb1 = base + n2 + hb1 * n3
        sb1 = base + n2 + n3 - hb1 * n3
        rb2 = rb1 + hb2 * n4
        sb2 = rb1 + n4 - hb2 * n4

        def add(r, n, land):
            def one(c, _):
                at = pl.ds(mo(r + c * n4), n4)
                got = land[pl.ds(mo(c * n4), n4)].astype(F32)
                g[a, at] = (g[a, at].astype(F32) + got).astype(BF16)
                return 0

            lax.fori_loop(0, n // n4, one, 0)

        c0 = send(rows(ga, other, n1), lc.at[i], core_dev)
        yield
        c0.wait_recv()
        add(base, n1, lc.at[i])
        c1 = send(rows(ga, sa1, n3), l1.at[i, 0], xa_dev)
        c2 = send(rows(ga, sb1, n3), l1.at[i, 1], xb_dev)
        yield
        c1.wait_recv()
        add(ra1, n3, l1.at[i, 0])
        c3 = send(rows(ga, sa2, n4), l2.at[i, 0], xb_dev)
        c2.wait_recv()
        add(rb1, n3, l1.at[i, 1])
        c4 = send(rows(ga, sb2, n4), l2.at[i, 1], xa_dev)
        yield
        c3.wait_recv()
        add(ra2, n4, l2.at[i, 0])
        c4.wait_recv()
        add(rb2, n4, l2.at[i, 1])
        c5 = send(rows(ga, ra2, n4), l3.at[i, 0], zlo_dev)
        c6 = send(rows(ga, rb2, n4), l3.at[i, 1], zlo_dev)
        yield
        for c, r, land in ((c5, ra2, l3.at[i, 0]), (c6, rb2, l3.at[i, 1])):
            c.wait_recv()
            both = g[a, pl.ds(mo(r), n4)].astype(F32) + land[...].astype(F32)
            fo[pl.ds(mo(r), n4)] = both.astype(BF16)
        c7 = send(rows(fo, ra2, n4), rows(fo, ra2, n4), xb_dev)
        c8 = send(rows(fo, rb2, n4), rows(fo, rb2, n4), xa_dev)
        yield
        c7.wait_recv()
        c9 = send(rows(fo, ra1, n3), rows(fo, ra1, n3), xa_dev)
        c8.wait_recv()
        c10 = send(rows(fo, rb1, n3), rows(fo, rb1, n3), xb_dev)
        yield
        c9.wait_recv()
        c10.wait_recv()
        c11 = send(rows(fo, base, n1), rows(fo, base, n1), core_dev)
        yield
        c11.wait_recv()

    def step(task):
        next(task, None)

    red = [reduce(i // 2, i % 2) for i in range(4)]
    sca = [[scatter(a, half) for half in range(2)] for a in range(2)]

    def activate():
        pre = by_panel(0)
        cdf = 0.5 * (1.0 + lax.erf(pre * 0.7071067811865476))
        hd[0, :NPAN] = (pre * cdf).astype(BF16).reshape(NPAN, 128, 128)
        slope_ref[...] = cdf + pre * jnp.exp(-0.5 * pre * pre) * 0.3989422804014327
        by_token(0)

    def differentiate():
        hd[1, :NPAN] = (by_panel(1) * slope_ref[...]).astype(BF16).reshape(NPAN, 128, 128)
        by_token(1)

    activate()
    arrive(1, 4)
    grads(0, 0)
    step(red[0])
    grads(0, 1)
    step(red[1])
    differentiate()
    partial(1, 0)
    partial(1, 1)
    step(red[0])
    step(sca[1][1])
    step(sca[1][0])
    grads(1, 0)
    grads(1, 1)
    step(red[3])
    step(red[1])
    step(red[2])
    partial(0, 1)
    step(sca[0][1])
    partial(0, 0)
    step(red[3])
    step(sca[0][0])
    step(red[0])
    step(sca[1][1])
    step(red[2])
    step(sca[1][0])
    step(red[1])
    step(sca[0][1])
    step(red[3])
    step(sca[0][0])
    step(red[0])
    step(sca[1][1])
    step(red[2])
    step(red[1])
    step(sca[1][0])
    step(red[3])
    step(sca[0][1])
    step(red[0])
    step(red[2])
    step(sca[0][0])
    step(red[1])
    step(sca[1][1])
    step(red[0])
    step(red[3])
    step(sca[1][0])
    step(sca[0][1])
    step(red[2])
    step(red[1])
    step(sca[0][0])
    step(red[0])
    step(sca[1][1])
    step(red[3])
    step(sca[1][0])
    step(red[2])
    step(sca[0][1])
    step(sca[0][0])
    step(red[1])
    step(red[0])
    step(red[3])
    step(sca[1][1])
    step(red[1])
    step(sca[1][0])
    step(red[2])
    step(red[3])
    step(sca[0][1])
    step(sca[0][0])
    step(red[2])
    for c in started:
        c.wait_send()


def copy_out(*refs):
    n = (len(refs) - 1) // 2
    copies = [pltpu.make_async_copy(refs[i], refs[n + i], refs[-1].at[i]) for i in range(n)]
    for c in copies:
        c.start()
    for c in copies:
        c.wait()


def near(value):
    return pltpu.with_memory_space_constraint(value, pltpu.VMEM)


def local(tokens, cotangent, w_in, w_out, in_rows, in_cols, out_rows, out_cols):
    smem = pl.BlockSpec(memory_space=pltpu.SMEM)
    hbm = pl.BlockSpec(memory_space=pl.ANY)
    vmem = pl.BlockSpec(memory_space=pltpu.VMEM)
    rows = tokens.shape[0]
    shapes = [(rows, D), (rows, D), (CAP * 128, 128), (CAP * 128, 128)]
    half = CAP * 64
    results = pl.pallas_call(
        kernel,
        out_shape=tuple(pltpu.VMEM(s, BF16) for s in shapes),
        in_specs=[hbm] * 4 + [smem] * 4,
        out_specs=(vmem,) * 4,
        scratch_shapes=[
            pltpu.VMEM((2, rows, D), BF16),
            pltpu.VMEM((2, NY, NZ, 16, 1024), BF16),
            pltpu.VMEM((2, NY, 16, D), BF16),
            pltpu.VMEM((2, 16, 1024), F32),
            pltpu.VMEM((2, 16, D), F32),
            pltpu.VMEM((16, D // 2), F32),
            pltpu.VMEM((NZ, 16, D // 8), F32),
            pltpu.VMEM((2, CAP + 1, 128, 128), BF16),
            pltpu.VMEM((2, 512, D), BF16),
            pltpu.VMEM((2, NCOL, 128, 128), BF16),
            pltpu.VMEM((2, NPAN + 1, 128, 128), BF16),
            pltpu.VMEM((2, 128, 512), BF16),
            pltpu.VMEM((2, 2, NY, 16, D // 2), BF16),
            pltpu.VMEM((2, 2, 4, 16, D // 2), BF16),
            pltpu.VMEM((2, 2, 4, 16, D // 2), BF16),
            pltpu.VMEM((2, 2, NZ, 16, D // 8), BF16),
            pltpu.VMEM((2, 2, NZ, 16, D // 8), BF16),
            pltpu.VMEM((2, CAP * 128, 128), BF16),
            pltpu.VMEM((4, half // 2, 128), BF16),
            pltpu.VMEM((4, 2, half // 8, 128), BF16),
            pltpu.VMEM((4, 2, half // 16, 128), BF16),
            pltpu.VMEM((4, 2, half // 16, 128), BF16),
            pltpu.VMEM((512, 128), F32),
            pltpu.VMEM((2, 8, 128), jnp.int32),
            pltpu.SMEM((2, 8, 128), jnp.int32),
            pltpu.SemaphoreType.DMA((SEMS,)),
            pltpu.SemaphoreType.DMA((SEMS,)),
            pltpu.SemaphoreType.DMA((5,)),
        ],
        compiler_params=pltpu.CompilerParams(
            collective_id=0, has_side_effects=True, vmem_limit_bytes=52 * 2**20
        ),
    )(tokens, cotangent, w_in, w_out, in_rows, in_cols, out_rows, out_cols)
    mixed, igrad, ing, outg = pl.pallas_call(
        copy_out,
        out_shape=tuple(jax.ShapeDtypeStruct(s, BF16) for s in shapes),
        in_specs=[vmem] * 4,
        out_specs=(hbm,) * 4,
        scratch_shapes=[pltpu.SemaphoreType.DMA((4,))],
        compiler_params=pltpu.CompilerParams(has_side_effects=True),
    )(*map(near, results))
    return mixed, igrad, ing.reshape(CAP, 128, 128), outg.reshape(CAP, 128, 128)


def solution(mesh):
    placed = (
        P(("dp", "fsdp"), None),
        P(("dp", "fsdp"), None),
        P("fsdp", None, None),
        P("fsdp", None, None),
        P("fsdp"),
        P("fsdp"),
        P("fsdp"),
        P("fsdp"),
    )
    return jax.shard_map(
        local,
        mesh=mesh,
        in_specs=placed,
        out_specs=(
            P(("dp", "fsdp"), None),
            P(("dp", "fsdp"), None),
            P("fsdp", None, None),
            P("fsdp", None, None),
        ),
        check_vma=False,
    )
```
